256 devices in a mesh: gx: 8 (over y, core), gy: 4 (over x), gz: 8 (over z).
Axes of the slice: x: 4, y: 4, z: 8, core: 2. Of those that a mesh axis runs over, the one named last changes fastest.
Arguments:
- tensor: float32 [4, 512, 512, 512], P(None, 'gx', 'gz', 'gy'), may hold values from -140 to 140, as said below
- starts: float32 [3, 512, 64], replicated, may hold values from -6 to 6
- trunc_ranks: int32 [3], replicated, may hold values from 32 to 64, as said below
Outputs:
- core_out: float32 [4, 64, 64, 64], P(None, ('gy', 'gz'), None, 'gx')
- factors: float32 [3, 512, 64], replicated
The draws below stay inside these ranges and needn't reach their ends.
Inputs may be any that keep to these rules, and one draw needn't show every extreme that they name: `trunc_ranks`: each rank lies between 32 and 64; at least one mode has rank 64. `tensor`: entries are bounded in magnitude by 140.
All inputs are finite; a program needn't handle non-finite values.
Results may differ from the reference program's by a relative error of at most 0.0003.
Values sent between devices are 32-bit elements; how exact they have to be, the bound alone decides.
No kernel may reach another device: no remote copies, remote signals or barrier semaphores. Data moves between devices by JAX's collectives and lax.ppermute only.
A program may use at most 128 MiB of HBM per device.

```python
import math
import jax
import jax.numpy as jnp
from jax import lax

N = 512
S = 4
RMAX = 64
RMIN = 32
ITERS = 4


def mode_scales(key, count, upper_scale):
    return jnp.exp(jax.random.uniform(key, (count,), jnp.float32, 0.0, math.log(upper_scale)))


def draw_tensor(key, part):
    key = jax.random.fold_in(key, 3)
    subkeys = jax.random.split(key, 5)
    noise_part = jnp.clip(jax.random.normal(subkeys[0], (S, N, N, N), jnp.float32), -6.0, 6.0)
    upper_scale = 2.0
    species_s = mode_scales(subkeys[1], S, upper_scale)
    first_s = mode_scales(subkeys[2], N, upper_scale)
    third_s = mode_scales(subkeys[3], N, upper_scale)
    second_s = mode_scales(subkeys[4], N, upper_scale)
    return (noise_part * species_s[:, None, None, None] * first_s[None, :, None, None] * third_s[None, None, :, None] * second_s[None, None, None, :]).astype(jnp.float32)


def draw_trunc_ranks(key, part):
    key = jax.random.fold_in(key, 7)
    subkeys = jax.random.split(key, 2)
    drawn = jax.random.randint(subkeys[0], (3,), RMIN, RMAX + 1)
    chosen = jax.random.randint(subkeys[1], (), 0, 3)
    return jnp.where(jnp.arange(3) == chosen, RMAX, drawn).astype(jnp.int32)


def noise(own_key, extent, width, reach, kind=jnp.bfloat16):
    return jnp.clip(width * jax.random.normal(own_key, extent, jnp.float32), -reach, reach).astype(kind)


def setup_inputs(seed: int = 0) -> dict:
    seeds = jax.random.split(jax.random.key(seed), 4)
    return {
        "tensor": draw_tensor(jax.random.fold_in(seeds[3], 71), 0),
        "starts": noise(seeds[1], (3, N, RMAX), 1.0, 6.0, jnp.float32),
        "trunc_ranks": draw_trunc_ranks(jax.random.fold_in(seeds[3], 71), 0),
    }


def orthonormal(gram_sum, start_cols):
    basis_now = start_cols
    for repeat in range(ITERS):
        image_cols = jnp.dot(gram_sum, basis_now, precision=lax.Precision.HIGHEST)
        inner_prod = jnp.dot(image_cols.T, image_cols, precision=lax.Precision.HIGHEST)
        lower_tri = jnp.linalg.cholesky(inner_prod)
        basis_now = lax.linalg.triangular_solve(lower_tri, image_cols, left_side=False, lower=True, transpose_a=True)
    return basis_now

def factor_from(gram_sum, start_cols, rank_now):
    keep_mask = (jnp.arange(RMAX, dtype=jnp.int32) < rank_now).astype(jnp.float32)
    return orthonormal(gram_sum, start_cols) * keep_mask[None, :]

def reference(tensor, starts, trunc_ranks):
    norm_scale = 1.0 / (S * N * N)
    high = lax.Precision.HIGHEST
    gram_one = jnp.einsum('sipq,sjpq->ij', tensor, tensor, precision=high) * norm_scale
    first_u = factor_from(gram_one, starts[0], trunc_ranks[0])
    shrunk_one = jnp.einsum('sipq,ir->srpq', tensor, first_u, precision=high)
    gram_two = jnp.einsum('spqi,spqj->ij', shrunk_one, shrunk_one, precision=high) * norm_scale
    second_u = factor_from(gram_two, starts[1], trunc_ranks[1])
    shrunk_two = jnp.einsum('spqi,ir->spqr', shrunk_one, second_u, precision=high)
    gram_three = jnp.einsum('spiq,spjq->ij', shrunk_two, shrunk_two, precision=high) * norm_scale
    third_u = factor_from(gram_three, starts[2], trunc_ranks[2])
    core_out = jnp.einsum('spiq,ir->sprq', shrunk_two, third_u, precision=high)
    return (core_out, jnp.stack([first_u, second_u, third_u]))
```

```python
import jax
import jax.numpy as jnp
from jax import lax
from jax.experimental import pallas as pl
from jax.experimental.pallas import tpu as pltpu
from jax.sharding import PartitionSpec as P

N = 512
R = 64
ITERS = 4
BF = jnp.bfloat16
F32 = jnp.float32
PAIRS = [(a, b) for a in range(4) for b in range(a, 4)]
NT = (((1,), (1,)), ((), ()))
NN = (((1,), (0,)), ((), ()))
VMEM = pl.BlockSpec(memory_space=pltpu.VMEM)
SMEM = pl.BlockSpec(memory_space=pltpu.SMEM)
ANY = pl.BlockSpec(memory_space=pl.ANY)


def split(x):
    hi = x.astype(BF)
    return hi, (x - hi.astype(F32)).astype(BF)


def mm(a, b, dims=NN):
    return lax.dot_general(a, b, dims, preferred_element_type=F32)


def put_blocks(out_ref, low, high):
    for n, (a, b) in enumerate(PAIRS):
        if a < 2:
            out_ref[n] = low[a * 128 : a * 128 + 128, b * 128 : b * 128 + 128]
        else:
            out_ref[n] = high[a * 128 - 256 : a * 128 - 128, b * 128 - 256 : b * 128 - 128]


def inverse_factor(cc):
    row8 = lax.broadcasted_iota(jnp.int32, (8, 128), 0)
    lane = lax.broadcasted_iota(jnp.int32, (8, 128), 1)
    m = [
        jnp.where(lane < R, (lane == row8 + 8 * b).astype(F32), cc[8 * b : 8 * b + 8, :])
        for b in range(8)
    ]
    scale = [jnp.ones((8, 128), F32) for _ in range(8)]
    for j0 in range(0, R, 4):
        b0 = j0 // 8
        cols = [
            [jnp.broadcast_to(m[b][:, R + j0 + k : R + j0 + k + 1], (8, 128)) for b in range(b0, 8)]
            for k in range(4)
        ]
        for k in range(4):
            r = (j0 + k) % 8
            pivot = cols[k][0][r : r + 1, :]
            inv = 1.0 / pivot
            scaled_row = m[b0][r : r + 1, :] * inv
            factors = [cols[k2][0][r : r + 1, :] * inv for k2 in range(k + 1, 4)]
            scale[b0] = jnp.where(row8 == r, pivot, scale[b0])
            for b in range(b0, 8):
                c = cols[k][b - b0]
                if b == b0:
                    c = jnp.where(row8 > r, c, 0.0)
                m[b] = m[b] - c * scaled_row
                for k2 in range(k + 1, 4):
                    cols[k2][b - b0] = cols[k2][b - b0] - c * factors[k2 - k - 1]
    out = []
    for b in range(8):
        y = lax.rsqrt(scale[b])
        y = y * (1.5 - 0.5 * (scale[b] * y) * y)
        out.append(m[b] * y)
    return jnp.concatenate(out, axis=0)


def subspace(gt_ref, start, gh_ref, gl_ref):
    for n, (a, b) in enumerate(PAIRS):
        blk = gt_ref[n]
        hi, lo = split(blk)
        gh_ref[a * 128 : a * 128 + 128, b * 128 : b * 128 + 128] = hi
        gl_ref[a * 128 : a * 128 + 128, b * 128 : b * 128 + 128] = lo
        if a != b:
            hi, lo = split(blk.T)
            gh_ref[b * 128 : b * 128 + 128, a * 128 : a * 128 + 128] = hi
            gl_ref[b * 128 : b * 128 + 128, a * 128 : a * 128 + 128] = lo

    lane = lax.broadcasted_iota(jnp.int32, (R, 128), 1)

    def step(_, v):
        vh, vl = split(v)
        t = mm(jnp.concatenate([vh, vl], axis=0), gh_ref[...])
        w = t[:R] + t[R:] + mm(vh, gl_ref[...])
        wh, wl = split(w)
        ws = jnp.concatenate([wh, wl], axis=0)
        c = mm(ws, ws, NT)
        c = c[:R] + c[R:]
        li = inverse_factor(c + pltpu.roll(c, R, 1))
        lh = li.astype(BF).astype(F32)
        both = jnp.where(lane < R, lh, pltpu.roll(li - lh, R, 1)).astype(BF)
        return mm(
            jnp.concatenate([both, both], axis=1),
            jnp.concatenate([wh, wh, wl, wl], axis=0),
        )

    return lax.fori_loop(0, ITERS, step, start)


def masked_factor(gt_ref, start_ref, rank_ref, mode, gh_ref, gl_ref, u_ref):
    v = subspace(gt_ref, start_ref[mode], gh_ref, gl_ref)
    row = lax.broadcasted_iota(jnp.int32, (R, N), 0)
    v = jnp.where(row < rank_ref[mode], v, 0.0)
    u_ref[...] = jnp.concatenate([v, v], axis=0).T[:, :R]
    return v


def gram_one_kernel(x_ref, g_ref, xh_ref, xl_ref, low_ref, high_ref):
    step = pl.program_id(0)

    @pl.when(step == 0)
    def _():
        low_ref[...] = jnp.zeros_like(low_ref)
        high_ref[...] = jnp.zeros_like(high_ref)

    for p in range(8):
        for g in range(8):
            hi, lo = split(x_ref[g, 0, pl.ds(p, 64, stride=8), :])
            xh_ref[p, g * 64 : g * 64 + 64, :] = hi
            xl_ref[p, g * 64 : g * 64 + 64, :] = lo
    for p in range(0, 8, 4):
        xh = jnp.concatenate([xh_ref[p + k] for k in range(4)], axis=1)
        xl = jnp.concatenate([xl_ref[p + k] for k in range(4)], axis=1)
        low_ref[...] += mm(xh[:256], xh, NT) + mm(xh[:256], xl, NT) + mm(xl[:256], xh, NT)
        high_ref[...] += (
            mm(xh[256:], xh[256:], NT) + mm(xh[256:], xl[256:], NT) + mm(xl[256:], xh[256:], NT)
        )

    @pl.when(step == pl.num_programs(0) - 1)
    def _():
        put_blocks(g_ref, low_ref[...] * 2.0**-20, high_ref[...] * 2.0**-20)


def gram_one(x):
    return pl.pallas_call(
        gram_one_kernel,
        grid=(4,),
        out_shape=(
            jax.ShapeDtypeStruct((10, 128, 128), F32),
            jax.ShapeDtypeStruct((8, N, N), BF),
            jax.ShapeDtypeStruct((8, N, N), BF),
        ),
        in_specs=[pl.BlockSpec((8, 1, N, 128), lambda i: (0, i, 0, 0))],
        out_specs=(
            pl.BlockSpec((10, 128, 128), lambda i: (0, 0, 0)),
            pl.BlockSpec((8, N, 128), lambda i: (0, 0, i)),
            pl.BlockSpec((8, N, 128), lambda i: (0, 0, i)),
        ),
        scratch_shapes=[pltpu.VMEM((256, N), F32), pltpu.VMEM((256, 256), F32)],
        compiler_params=pltpu.CompilerParams(vmem_limit_bytes=40 * 2**20),
        name="gram_one",
    )(x)


def factor_one_kernel(
    gt_ref, start_ref, rank_ref, xh_hbm, xl_hbm, u_ref, a_ref, g_ref, gh_ref, gl_ref, xh_ref, xl_ref, sem
):
    copies = [
        pltpu.make_async_copy(xh_hbm, xh_ref, sem.at[0]),
        pltpu.make_async_copy(xl_hbm, xl_ref, sem.at[1]),
    ]
    for c in copies:
        c.start()
    v = masked_factor(gt_ref, start_ref, rank_ref, 0, gh_ref, gl_ref, u_ref)
    vh, vl = split(v)
    vs = jnp.concatenate([vh, vl], axis=0)
    for c in copies:
        c.wait()
    for p in range(8):
        t = mm(vs, xh_ref[p])
        y = t[:R] + t[R:] + mm(vh, xl_ref[p])
        for q in range(4):
            a_ref[q, pl.ds(p, R, stride=8), :] = y[:, 128 * q : 128 * q + 128]
    a = jnp.concatenate([a_ref[q] for q in range(4)], axis=1)
    ah, al = split(a)
    th, tl = split(a.T)
    low = mm(th[:256], ah) + mm(th[:256], al) + mm(tl[:256], ah)
    high = mm(th[256:], ah[:, 256:]) + mm(th[256:], al[:, 256:]) + mm(tl[256:], ah[:, 256:])
    put_blocks(g_ref, low * 2.0**-20, high * 2.0**-20)


def factor_one(gt, starts, ranks, xh, xl):
    return pl.pallas_call(
        factor_one_kernel,
        out_shape=(
            jax.ShapeDtypeStruct((N, R), F32),
            jax.ShapeDtypeStruct((4, N, 128), F32),
            jax.ShapeDtypeStruct((10, 128, 128), F32),
        ),
        in_specs=[VMEM, VMEM, SMEM, ANY, ANY],
        out_specs=(VMEM, VMEM, VMEM),
        scratch_shapes=[
            pltpu.VMEM((N, N), BF),
            pltpu.VMEM((N, N), BF),
            pltpu.VMEM((8, N, N), BF),
            pltpu.VMEM((8, N, N), BF),
            pltpu.SemaphoreType.DMA((2,)),
        ],
        compiler_params=pltpu.CompilerParams(vmem_limit_bytes=40 * 2**20),
        name="factor_one",
    )(gt, starts, ranks, xh, xl)


def factor_two_kernel(gt_ref, start_ref, rank_ref, a_ref, u_ref, y_ref, gh_ref, gl_ref):
    v = masked_factor(gt_ref, start_ref, rank_ref, 1, gh_ref, gl_ref, u_ref)
    vh, vl = split(v)
    vs = jnp.concatenate([vh, vl], axis=0)
    ah, al = split(jnp.concatenate([a_ref[q] for q in range(4)], axis=1))
    y = mm(ah, vs, NT) + mm(al, vs, NT)
    y = y + pltpu.roll(y, R, 1)
    rolled = [y if k == 0 else pltpu.roll(y, 8 * k, 1) for k in range(8)]
    group = lax.broadcasted_iota(jnp.int32, (8, 128), 1) // 8
    for bx in range(8):
        for by in range(4):
            tile = jnp.zeros((8, 128), F32)
            for r in range(16):
                at = (by * 16 + r) * 8
                tile = jnp.where(group == r, rolled[(r - bx) % 8][at : at + 8, :], tile)
            y_ref[bx * 4 + by] = tile


def factor_two(gt, starts, ranks, a):
    return pl.pallas_call(
        factor_two_kernel,
        out_shape=(
            jax.ShapeDtypeStruct((N, R), F32),
            jax.ShapeDtypeStruct((32, 8, 128), F32),
        ),
        in_specs=[VMEM, VMEM, SMEM, VMEM],
        out_specs=(VMEM, VMEM),
        scratch_shapes=[pltpu.VMEM((N, N), BF), pltpu.VMEM((N, N), BF)],
        compiler_params=pltpu.CompilerParams(vmem_limit_bytes=32 * 2**20),
        name="factor_two",
    )(gt, starts, ranks, a)


def columns(b_ref):
    return jnp.concatenate(
        [b_ref[:, 8 * s : 8 * s + 8].reshape(N, 128) for s in range(4)], axis=1
    )


def gram_three_kernel(b_ref, g_ref):
    bh, bl = split(columns(b_ref))
    low = mm(bh[:256], bh, NT) + mm(bh[:256], bl, NT) + mm(bl[:256], bh, NT)
    high = mm(bh[256:], bh[256:], NT) + mm(bh[256:], bl[256:], NT) + mm(bl[256:], bh[256:], NT)
    put_blocks(g_ref, low * 2.0**-20, high * 2.0**-20)


def gram_three(b):
    return pl.pallas_call(
        gram_three_kernel,
        out_shape=jax.ShapeDtypeStruct((10, 128, 128), F32),
        in_specs=[VMEM],
        out_specs=VMEM,
        compiler_params=pltpu.CompilerParams(vmem_limit_bytes=32 * 2**20),
        name="gram_three",
    )(b)


def factor_three_kernel(gt_ref, start_ref, rank_ref, place_ref, b_ref, u_ref, core_ref, gh_ref, gl_ref):
    v = masked_factor(gt_ref, start_ref, rank_ref, 2, gh_ref, gl_ref, u_ref)
    vh, vl = split(v)
    bh, bl = split(columns(b_ref))
    t = mm(jnp.concatenate([vh, vl], axis=0), bh)
    core = t[:R] + t[R:] + mm(vh, bl)
    shift = (8 - place_ref[0]) * 16
    for s in range(4):
        part = pltpu.roll(core[:, s * 128 : s * 128 + 128], shift, 1)
        core_ref[s, 0] = part[:, 0:8]
        core_ref[s, 1] = part[:, 8:16]


def factor_three(gt, starts, ranks, place, b):
    return pl.pallas_call(
        factor_three_kernel,
        out_shape=(
            jax.ShapeDtypeStruct((N, R), F32),
            jax.ShapeDtypeStruct((4, 2, R, 8), F32),
        ),
        in_specs=[VMEM, VMEM, SMEM, SMEM, VMEM],
        out_specs=(VMEM, VMEM),
        scratch_shapes=[pltpu.VMEM((N, N), BF), pltpu.VMEM((N, N), BF)],
        compiler_params=pltpu.CompilerParams(vmem_limit_bytes=32 * 2**20),
        name="factor_three",
    )(gt, starts, ranks, place, b)


PLANE = ("gx", "gy")


def swap(x, axes):
    return lax.all_to_all(x, axes, 0, 0, tiled=True)


def spread(x, axes, count):
    return swap(jnp.broadcast_to(x[None], (count,) + x.shape), axes)


def sum_plane(g):
    return jnp.sum(swap(g.reshape(32, 40, 128), PLANE), axis=0)


def local(tensor, starts, trunc_ranks):
    starts_t = jnp.swapaxes(starts, 1, 2)
    place = lax.axis_index("gz").astype(jnp.int32).reshape(1)
    x = tensor.reshape(4, 64, 8, 8, 128).transpose(0, 2, 1, 3, 4).reshape(32, N, 128)
    x = swap(x, PLANE).reshape(8, 4, N, 128)
    g, xh, xl = gram_one(x)
    g = jnp.sum(spread(sum_plane(g), "gz", 8), axis=0)
    g = spread(g, PLANE, 32).reshape(10, 128, 128)
    u_one, a, g = factor_one(g, starts_t, trunc_ranks, xh, xl)
    g = jnp.sum(spread(sum_plane(g), "gz", 8), axis=0)
    g = spread(g, PLANE, 32).reshape(10, 128, 128)
    u_two, y = factor_two(g, starts_t, trunc_ranks, a)
    b = spread(swap(y, PLANE), "gz", 8)
    g = sum_plane(gram_three(b))
    g = spread(g, PLANE, 32).reshape(10, 128, 128)
    u_three, core_out = factor_three(g, starts_t, trunc_ranks, place, b)
    return (core_out, jnp.stack([u_one, u_two, u_three]))


def solution(mesh):
    return jax.shard_map(
        local,
        mesh=mesh,
        in_specs=(P(None, "gx", "gz", "gy"), P(), P()),
        out_specs=(P(None, ("gy", "gz"), None, "gx"), P()),
        check_vma=False,
    )
```

```python
import jax
import jax.numpy as jnp
from jax import lax
from jax.experimental import pallas as pl
from jax.experimental.pallas import tpu as pltpu
from jax.sharding import PartitionSpec as P

N = 512
R = 64
ITERS = 4
BF = jnp.bfloat16
F32 = jnp.float32
PAIRS = [(a, b) for a in range(4) for b in range(a, 4)]
NT = (((1,), (1,)), ((), ()))
NN = (((1,), (0,)), ((), ()))
VMEM = pl.BlockSpec(memory_space=pltpu.VMEM)
SMEM = pl.BlockSpec(memory_space=pltpu.SMEM)
HBM = pl.BlockSpec(memory_space=pltpu.HBM)


def split(x):
    hi = x.astype(BF)
    return hi, (x - hi.astype(F32)).astype(BF)


def mm(a, b, dims=NN):
    return lax.dot_general(a, b, dims, preferred_element_type=F32)


def put_blocks(keep_ref, send_ref, core, low, high):
    for here in range(2):

        @pl.when(core == here)
        def _():
            for n, (a, b) in enumerate(PAIRS):
                out_ref = keep_ref if n // 5 == here else send_ref
                if a < 2:
                    out_ref[n % 5] = low[a * 128 : a * 128 + 128, b * 128 : b * 128 + 128]
                else:
                    out_ref[n % 5] = high[a * 128 - 256 : a * 128 - 128, b * 128 - 256 : b * 128 - 128]


HALF = jax.ShapeDtypeStruct((5, 128, 128), F32)


def inverse_factor(cc):
    row8 = lax.broadcasted_iota(jnp.int32, (8, 128), 0)
    lane = lax.broadcasted_iota(jnp.int32, (8, 128), 1)
    m = [
        jnp.where(lane < R, (lane == row8 + 8 * b).astype(F32), cc[8 * b : 8 * b + 8, :])
        for b in range(8)
    ]
    scale = [jnp.ones((8, 128), F32) for _ in range(8)]
    for b0 in range(8):
        cols = [
            [jnp.broadcast_to(m[b][:, R + 8 * b0 + k : R + 8 * b0 + k + 1], (8, 128)) for b in range(b0, 8)]
            for k in range(8)
        ]
        for k in range(8):
            pivot = cols[k][0][k : k + 1, :]
            inv = 1.0 / pivot
            scaled_row = m[b0][k : k + 1, :] * inv
            factors = [cols[k2][0][k : k + 1, :] * inv for k2 in range(k + 1, 8)]
            scale[b0] = jnp.where(row8 == k, pivot, scale[b0])
            for b in range(b0, 8):
                c = cols[k][b - b0]
                if b == b0:
                    c = jnp.where(row8 > k, c, 0.0)
                m[b] = m[b] - c * scaled_row
                for k2 in range(k + 1, 8):
                    cols[k2][b - b0] = cols[k2][b - b0] - c * factors[k2 - k - 1]
    out = []
    for b in range(8):
        y = lax.rsqrt(scale[b])
        y = y * (1.5 - 0.5 * (scale[b] * y) * y)
        out.append(m[b] * y)
    return jnp.concatenate(out, axis=0)


def subspace(halves, core, start, gh_ref, gl_ref):
    for here in range(2):

        @pl.when(core == here)
        def _():
            for n, (a, b) in enumerate(PAIRS):
                blk = halves[(n // 5 + here) % 2][n % 5]
                hi, lo = split(blk)
                gh_ref[a * 128 : a * 128 + 128, b * 128 : b * 128 + 128] = hi
                gl_ref[a * 128 : a * 128 + 128, b * 128 : b * 128 + 128] = lo
                if a != b:
                    hi, lo = split(blk.T)
                    gh_ref[b * 128 : b * 128 + 128, a * 128 : a * 128 + 128] = hi
                    gl_ref[b * 128 : b * 128 + 128, a * 128 : a * 128 + 128] = lo

    lane = lax.broadcasted_iota(jnp.int32, (R, 128), 1)

    def image(vh, vs):
        t = mm(vs, gh_ref[...])
        return t[:R] + t[R:] + mm(vh, gl_ref[...])

    def step(k, w):
        wh, wl = split(w)
        ws = jnp.concatenate([wh, wl], axis=0)
        c = mm(ws, ws, NT)
        c = c[:R] + c[R:]
        z = jnp.where(k == ITERS - 1, w, image(wh, ws))
        zh, zl = split(z)
        li = inverse_factor(c + pltpu.roll(c, R, 1))
        lh = li.astype(BF).astype(F32)
        both = jnp.where(lane < R, lh, pltpu.roll(li - lh, R, 1)).astype(BF)
        return mm(
            jnp.concatenate([both, both], axis=1),
            jnp.concatenate([zh, zh, zl, zl], axis=0),
        )

    vh, vl = split(start)
    return lax.fori_loop(0, ITERS, step, image(vh, jnp.concatenate([vh, vl], axis=0)))


def masked_factor(halves, start_ref, rank_ref, place_ref, mode, gh_ref, gl_ref):
    v = subspace(halves, place_ref[0], start_ref[mode], gh_ref, gl_ref)
    row = lax.broadcasted_iota(jnp.int32, (R, N), 0)
    return jnp.where(row < rank_ref[mode], v, 0.0)


def gram_one_kernel(place_ref, x_ref, keep_ref, send_ref, x2_ref, low_ref, high_ref):
    step = pl.program_id(0)

    @pl.when(step == 0)
    def _():
        low_ref[...] = jnp.zeros_like(low_ref)
        high_ref[...] = jnp.zeros_like(high_ref)

    for p in range(8):
        for g in range(8):
            hi, lo = split(x_ref[g, 0, pl.ds(p, 64, stride=8), :])
            x2_ref[0, p, g * 64 : g * 64 + 64, :] = hi
            x2_ref[1, p, g * 64 : g * 64 + 64, :] = lo
    for p in range(0, 8, 4):
        xh = jnp.concatenate([x2_ref[0, p + k] for k in range(4)], axis=1)
        xl = jnp.concatenate([x2_ref[1, p + k] for k in range(4)], axis=1)
        low_ref[...] += mm(xh[:256], xh, NT) + mm(xh[:256], xl, NT) + mm(xl[:256], xh, NT)
        high_ref[...] += (
            mm(xh[256:], xh[256:], NT) + mm(xh[256:], xl[256:], NT) + mm(xl[256:], xh[256:], NT)
        )

    @pl.when(step == pl.num_programs(0) - 1)
    def _():
        put_blocks(keep_ref, send_ref, place_ref[0], low_ref[...] * 2.0**-20, high_ref[...] * 2.0**-20)


def gram_one(place, x):
    half = pl.BlockSpec((5, 128, 128), lambda i: (0, 0, 0))
    return pl.pallas_call(
        gram_one_kernel,
        grid=(4,),
        out_shape=(HALF, HALF, pltpu.HBM((2, 8, N, N), BF)),
        in_specs=[SMEM, pl.BlockSpec((8, 1, N, 128), lambda i: (0, i, 0, 0))],
        out_specs=(half, half, pl.BlockSpec((2, 8, N, 128), lambda i: (0, 0, 0, i))),
        scratch_shapes=[pltpu.VMEM((256, N), F32), pltpu.VMEM((256, 256), F32)],
        compiler_params=pltpu.CompilerParams(vmem_limit_bytes=40 * 2**20),
        name="gram_one",
    )(place, x)


def factor_one_kernel(
    mine_ref, other_ref, start_ref, rank_ref, place_ref, x_hbm, u_ref, a_ref, keep_ref, send_ref, gh_ref, gl_ref, x_ref, sem
):
    copy = pltpu.make_async_copy(x_hbm, x_ref, sem)
    copy.start()
    v = masked_factor((mine_ref, other_ref), start_ref, rank_ref, place_ref, 0, gh_ref, gl_ref)
    u_ref[...] = v
    vh, vl = split(v)
    vs = jnp.concatenate([vh, vl], axis=0)
    copy.wait()
    for p in range(8):
        t = mm(vs, x_ref[0, p])
        y = t[:R] + t[R:] + mm(vh, x_ref[1, p])
        for q in range(4):
            a_ref[q, pl.ds(p, R, stride=8), :] = y[:, 128 * q : 128 * q + 128]
    a = jnp.concatenate([a_ref[q] for q in range(4)], axis=1)
    ah, al = split(a)
    th, tl = split(a.T)
    low = mm(th[:256], ah) + mm(th[:256], al) + mm(tl[:256], ah)
    high = mm(th[256:], ah[:, 256:]) + mm(th[256:], al[:, 256:]) + mm(tl[256:], ah[:, 256:])
    put_blocks(keep_ref, send_ref, place_ref[0], low * 2.0**-20, high * 2.0**-20)


def factor_one(halves, starts, ranks, place, x2):
    return pl.pallas_call(
        factor_one_kernel,
        out_shape=(
            jax.ShapeDtypeStruct((R, N), F32),
            jax.ShapeDtypeStruct((4, N, 128), F32),
            HALF,
            HALF,
        ),
        in_specs=[VMEM, VMEM, VMEM, SMEM, SMEM, HBM],
        out_specs=(VMEM,) * 4,
        scratch_shapes=[
            pltpu.VMEM((N, N), BF),
            pltpu.VMEM((N, N), BF),
            pltpu.VMEM((2, 8, N, N), BF),
            pltpu.SemaphoreType.DMA,
        ],
        compiler_params=pltpu.CompilerParams(vmem_limit_bytes=53 * 2**20),
        name="factor_one",
    )(*halves, starts, ranks, place, x2)


def factor_two_kernel(mine_ref, other_ref, start_ref, rank_ref, place_ref, a_ref, u_ref, y_ref, gh_ref, gl_ref):
    v = masked_factor((mine_ref, other_ref), start_ref, rank_ref, place_ref, 1, gh_ref, gl_ref)
    u_ref[...] = v
    vh, vl = split(v)
    vs = jnp.concatenate([vh, vl], axis=0)
    ah, al = split(jnp.concatenate([a_ref[q] for q in range(4)], axis=1))
    y = mm(ah, vs, NT) + mm(al, vs, NT)
    y = y + pltpu.roll(y, R, 1)
    rolled = [y if k == 0 else pltpu.roll(y, 8 * k, 1) for k in range(8)]
    group = lax.broadcasted_iota(jnp.int32, (8, 128), 1) // 8
    for bx in range(8):
        for by in range(4):
            tile = jnp.zeros((8, 128), F32)
            for r in range(16):
                at = (by * 16 + r) * 8
                tile = jnp.where(group == r, rolled[(r - bx) % 8][at : at + 8, :], tile)
            y_ref[bx * 4 + by] = tile


def factor_two(halves, starts, ranks, place, a):
    return pl.pallas_call(
        factor_two_kernel,
        out_shape=(
            jax.ShapeDtypeStruct((R, N), F32),
            jax.ShapeDtypeStruct((32, 8, 128), F32),
        ),
        in_specs=[VMEM, VMEM, VMEM, SMEM, SMEM, VMEM],
        out_specs=(VMEM, VMEM),
        scratch_shapes=[pltpu.VMEM((N, N), BF), pltpu.VMEM((N, N), BF)],
        compiler_params=pltpu.CompilerParams(vmem_limit_bytes=32 * 2**20),
        name="factor_two",
    )(*halves, starts, ranks, place, a)


def pack_kernel(y_ref, out_ref):
    group = lax.broadcasted_iota(jnp.int32, (32, 128), 1) // 16
    for z in range(8):
        rows = jnp.zeros((32, 128), F32)
        for g in range(8):
            at = 8 * (g % 4) + 4 * (g // 4)
            tile = y_ref[at : at + 4].reshape(32, 128)
            if g != z:
                tile = pltpu.roll(tile, (16 * (g - z)) % 128, 1)
            rows = jnp.where(group == g, tile, rows)
        out_ref[z] = rows


def pack(y):
    return pl.pallas_call(
        pack_kernel,
        out_shape=jax.ShapeDtypeStruct((8, 32, 128), F32),
        in_specs=[VMEM],
        out_specs=VMEM,
        name="pack",
    )(y)


def gram_three_kernel(place_ref, y_ref, keep_ref, send_ref, b_ref):
    lane = lax.broadcasted_iota(jnp.int32, (32, 128), 1)
    for z in range(8):
        y = y_ref[z]
        b_ref[64 * z : 64 * z + 32, :] = jnp.where(lane < R, y, 0.0)
        b_ref[64 * z + 32 : 64 * z + 64, :] = jnp.where(lane < R, pltpu.roll(y, R, 1), 0.0)
    bh, bl = split(b_ref[...])
    low = mm(bh[:256], bh, NT) + mm(bh[:256], bl, NT) + mm(bl[:256], bh, NT)
    high = mm(bh[256:], bh[256:], NT) + mm(bh[256:], bl[256:], NT) + mm(bl[256:], bh[256:], NT)
    put_blocks(keep_ref, send_ref, place_ref[0], low * 2.0**-20, high * 2.0**-20)


def gram_three(place, y):
    return pl.pallas_call(
        gram_three_kernel,
        out_shape=(HALF, HALF, jax.ShapeDtypeStruct((N, 128), F32)),
        in_specs=[SMEM, VMEM],
        out_specs=(VMEM, VMEM, VMEM),
        compiler_params=pltpu.CompilerParams(vmem_limit_bytes=32 * 2**20),
        name="gram_three",
    )(place, y)


def factor_three_kernel(
    mine_ref, other_ref, start_ref, rank_ref, place_ref, b_ref, u_one_ref, u_two_ref, u_ref, core_ref, gh_ref, gl_ref
):
    v = masked_factor((mine_ref, other_ref), start_ref, rank_ref, place_ref, 2, gh_ref, gl_ref)
    u_ref[0] = u_one_ref[...]
    u_ref[1] = u_two_ref[...]
    u_ref[2] = v
    vh, vl = split(v)
    bh, bl = split(b_ref[...])
    t = mm(jnp.concatenate([vh, vl], axis=0), bh)
    core = t[:R] + t[R:] + mm(vh, bl)
    core = jnp.concatenate([core, core], axis=0).T
    for s in range(4):
        for e in range(2):
            core_ref[s, e] = core[16 * s + 8 * e : 16 * s + 8 * e + 8, :R]


def factor_three(halves, starts, ranks, place, b, u_one, u_two):
    return pl.pallas_call(
        factor_three_kernel,
        out_shape=(
            jax.ShapeDtypeStruct((3, R, N), F32),
            jax.ShapeDtypeStruct((4, 2, 8, R), F32),
        ),
        in_specs=[VMEM, VMEM, VMEM, SMEM, SMEM, VMEM, VMEM, VMEM],
        out_specs=(VMEM, VMEM),
        scratch_shapes=[pltpu.VMEM((N, N), BF), pltpu.VMEM((N, N), BF)],
        compiler_params=pltpu.CompilerParams(vmem_limit_bytes=32 * 2**20),
        name="factor_three",
    )(*halves, starts, ranks, place, b, u_one, u_two)


PLANE = ("y", "gy")


def swap(x, axes):
    return lax.all_to_all(x, axes, 0, 0, tiled=True)


def spread(x, axes, count):
    return swap(jnp.broadcast_to(x[None], (count,) + x.shape), axes)


def other_core(x):
    return lax.ppermute(x, "core", [(0, 1), (1, 0)])


def total(keep, send):
    g = keep + other_core(send)
    g = jnp.sum(swap(g.reshape(16, 40, 128), PLANE), axis=0)
    g = jnp.sum(spread(g, "gz", 8), axis=0)
    g = spread(g, PLANE, 16).reshape(5, 128, 128)
    return g, other_core(g)


def local(tensor, starts, trunc_ranks):
    starts_t = jnp.swapaxes(starts, 1, 2)
    place = lax.axis_index("core").astype(jnp.int32).reshape(1)
    tensor, place = lax.optimization_barrier((tensor, place))
    x = tensor.reshape(4, 64, 8, 8, 128).transpose(0, 2, 1, 3, 4).reshape(32, N, 128)
    x = swap(x, ("y", "core", "gy")).reshape(8, 4, N, 128)
    keep, send, x2 = gram_one(place, x)
    u_one, a, keep, send = factor_one(total(keep, send), starts_t, trunc_ranks, place, x2)
    u_two, y = factor_two(total(keep, send), starts_t, trunc_ranks, place, a)
    y = pack(swap(y, ("y", "core", "gy")))
    keep, send, b = gram_three(place, swap(y, "gz"))
    factors, core_out = factor_three(total(keep, send), starts_t, trunc_ranks, place, b, u_one, u_two)
    return (jnp.swapaxes(core_out, 2, 3), jnp.swapaxes(factors, 1, 2))


def solution(mesh):
    fine = jax.sharding.Mesh(mesh.devices.reshape(4, 2, 4, 8), ("y", "core", "gy", "gz"))
    gx = ("y", "core")
    return jax.shard_map(
        local,
        mesh=fine,
        in_specs=(P(None, gx, "gz", "gy"), P(), P()),
        out_specs=(P(None, ("gy", "gz"), None, gx), P()),
        check_vma=False,
    )
```

```python
import jax
import jax.numpy as jnp
from jax import lax
from jax.experimental import pallas as pl
from jax.experimental.pallas import tpu as pltpu
from jax.sharding import PartitionSpec as P

N = 512
R = 64
ITERS = 4
BF = jnp.bfloat16
F32 = jnp.float32
PAIRS = [(a, b) for a in range(4) for b in range(a, 4)]
NT = (((1,), (1,)), ((), ()))
NN = (((1,), (0,)), ((), ()))
VMEM = pl.BlockSpec(memory_space=pltpu.VMEM)
SMEM = pl.BlockSpec(memory_space=pltpu.SMEM)
HBM = pl.BlockSpec(memory_space=pltpu.HBM)


def split(x):
    hi = x.astype(BF)
    return hi, (x - hi.astype(F32)).astype(BF)


def mm(a, b, dims=NN):
    return lax.dot_general(a, b, dims, preferred_element_type=F32)


def put_blocks(keep_ref, send_ref, core, low, high):
    for here in range(2):

        @pl.when(core == here)
        def _():
            for n, (a, b) in enumerate(PAIRS):
                out_ref = keep_ref if n // 5 == here else send_ref
                if a < 2:
                    out_ref[n % 5] = low[a * 128 : a * 128 + 128, b * 128 : b * 128 + 128]
                else:
                    out_ref[n % 5] = high[a * 128 - 256 : a * 128 - 128, b * 128 - 256 : b * 128 - 128]


HALF = jax.ShapeDtypeStruct((5, 128, 128), F32)


def column(x, j):
    return jnp.broadcast_to(x[:, R + j : R + j + 1], (8, 128))


def row(x, k):
    return jnp.broadcast_to(x[k : k + 1, :], (8, 128))


def inverse_factor(cc):
    row8 = lax.broadcasted_iota(jnp.int32, (8, 128), 0)
    lane = lax.broadcasted_iota(jnp.int32, (8, 128), 1)
    m = [
        jnp.where(lane < R, (lane == row8 + 8 * b).astype(F32), cc[8 * b : 8 * b + 8, :])
        for b in range(8)
    ]
    scale = []
    diag = [column(m[0], k) for k in range(8)]
    for b0 in range(8):
        below = [[column(m[b], 8 * b0 + k) for b in range(b0 + 1, 8)] for k in range(8)]
        ahead = [column(m[b0 + 1], 8 * b0 + 8 + k) for k in range(8)] if b0 < 7 else []
        pivots = jnp.ones((8, 128), F32)
        for k in range(8):
            pivot = row(diag[k], k)
            inv = 1.0 / pivot
            scaled_row = row(m[b0], k) * inv
            rest = jnp.where(row8 > k, diag[k], 0.0)
            pivots = jnp.where(row8 == k, pivot, pivots)
            factors = {k2: row(diag[k2], k) * inv for k2 in range(k + 1, 8)}
            for k2 in factors:
                diag[k2] = diag[k2] - rest * factors[k2]
            m[b0] = m[b0] - rest * scaled_row
            for n in range(7 - b0):
                m[b0 + 1 + n] = m[b0 + 1 + n] - below[k][n] * scaled_row
                for k2 in factors:
                    below[k2][n] = below[k2][n] - below[k][n] * factors[k2]
            for k2 in range(len(ahead)):
                ahead[k2] = ahead[k2] - below[k][0] * (row(below[k][0], k2) * inv)
        scale.append(pivots)
        diag = ahead
    out = []
    for b in range(8):
        y = lax.rsqrt(scale[b])
        y = y * (1.5 - 0.5 * (scale[b] * y) * y)
        out.append(m[b] * y)
    return jnp.concatenate(out, axis=0)


def subspace(halves, core, start, gh_ref, gl_ref):
    for here in range(2):

        @pl.when(core == here)
        def _():
            for n, (a, b) in enumerate(PAIRS):
                blk = halves[(n // 5 + here) % 2][n % 5]
                hi, lo = split(blk)
                gh_ref[a * 128 : a * 128 + 128, b * 128 : b * 128 + 128] = hi
                gl_ref[a * 128 : a * 128 + 128, b * 128 : b * 128 + 128] = lo
                if a != b:
                    hi, lo = split(blk.T)
                    gh_ref[b * 128 : b * 128 + 128, a * 128 : a * 128 + 128] = hi
                    gl_ref[b * 128 : b * 128 + 128, a * 128 : a * 128 + 128] = lo

    lane = lax.broadcasted_iota(jnp.int32, (R, 128), 1)

    def image(vh, vs):
        t = mm(vs, gh_ref[...])
        return t[:R] + t[R:] + mm(vh, gl_ref[...])

    def step(k, w):
        wh, wl = split(w)
        ws = jnp.concatenate([wh, wl], axis=0)
        c = mm(ws, ws, NT)
        c = c[:R] + c[R:]
        z = jnp.where(k == ITERS - 1, w, image(wh, ws))
        zh, zl = split(z)
        li = inverse_factor(c + pltpu.roll(c, R, 1))
        lh = li.astype(BF).astype(F32)
        both = jnp.where(lane < R, lh, pltpu.roll(li - lh, R, 1)).astype(BF)
        return mm(
            jnp.concatenate([both, both], axis=1),
            jnp.concatenate([zh, zh, zl, zl], axis=0),
        )

    vh, vl = split(start)
    return lax.fori_loop(0, ITERS, step, image(vh, jnp.concatenate([vh, vl], axis=0)))


def masked_factor(halves, start_ref, rank_ref, place_ref, mode, gh_ref, gl_ref):
    v = subspace(halves, place_ref[0], start_ref[mode], gh_ref, gl_ref)
    index = lax.broadcasted_iota(jnp.int32, (R, N), 0)
    return jnp.where(index < rank_ref[mode], v, 0.0)


def gram_one_kernel(place_ref, x_ref, keep_ref, send_ref, x2_ref, low_ref, high_ref, cross_ref):
    step = pl.program_id(0)

    @pl.when(step == 0)
    def _():
        low_ref[...] = jnp.zeros_like(low_ref)
        high_ref[...] = jnp.zeros_like(high_ref)
        cross_ref[...] = jnp.zeros_like(cross_ref)

    for p in range(8):
        for g in range(8):
            hi, lo = split(x_ref[g, 0, pl.ds(p, 64, stride=8), :])
            x2_ref[0, p, g * 64 : g * 64 + 64, :] = hi
            x2_ref[1, p, g * 64 : g * 64 + 64, :] = lo
    for p in range(0, 8, 4):
        xh = jnp.concatenate([x2_ref[0, p + k] for k in range(4)], axis=1)
        xl = jnp.concatenate([x2_ref[1, p + k] for k in range(4)], axis=1)
        low_ref[...] += mm(xh[:256], xh, NT)
        high_ref[...] += mm(xh[256:], xh[256:], NT)
        cross_ref[...] += mm(xh, xl, NT)

    @pl.when(step == pl.num_programs(0) - 1)
    def _():
        cross = cross_ref[...]
        cross = cross + cross.T
        low = low_ref[...] + cross[:256]
        high = high_ref[...] + cross[256:, 256:]
        put_blocks(keep_ref, send_ref, place_ref[0], low * 2.0**-20, high * 2.0**-20)


def gram_one(place, x):
    half = pl.BlockSpec((5, 128, 128), lambda i: (0, 0, 0))
    return pl.pallas_call(
        gram_one_kernel,
        grid=(4,),
        out_shape=(HALF, HALF, pltpu.HBM((2, 8, N, N), BF)),
        in_specs=[SMEM, pl.BlockSpec((8, 1, N, 128), lambda i: (0, i, 0, 0))],
        out_specs=(half, half, pl.BlockSpec((2, 8, N, 128), lambda i: (0, 0, 0, i))),
        scratch_shapes=[pltpu.VMEM((256, N), F32), pltpu.VMEM((256, 256), F32), pltpu.VMEM((N, N), F32)],
        compiler_params=pltpu.CompilerParams(vmem_limit_bytes=40 * 2**20),
        name="gram_one",
    )(place, x)


def factor_one_kernel(
    mine_ref, other_ref, start_ref, rank_ref, place_ref, x_hbm, u_ref, a_ref, keep_ref, send_ref, gh_ref, gl_ref, x_ref, sem
):
    copy = pltpu.make_async_copy(x_hbm, x_ref, sem)
    copy.start()
    v = masked_factor((mine_ref, other_ref), start_ref, rank_ref, place_ref, 0, gh_ref, gl_ref)
    u_ref[...] = v
    vh, vl = split(v)
    vs = jnp.concatenate([vh, vl], axis=0)
    copy.wait()
    for p in range(8):
        t = mm(vs, x_ref[0, p])
        y = t[:R] + t[R:] + mm(vh, x_ref[1, p])
        for q in range(4):
            a_ref[q, pl.ds(p, R, stride=8), :] = y[:, 128 * q : 128 * q + 128]
    a = jnp.concatenate([a_ref[q] for q in range(4)], axis=1)
    ah, al = split(a)
    th, tl = split(a.T)
    low = mm(th[:256], ah) + mm(th[:256], al) + mm(tl[:256], ah)
    high = mm(th[256:], ah[:, 256:]) + mm(th[256:], al[:, 256:]) + mm(tl[256:], ah[:, 256:])
    put_blocks(keep_ref, send_ref, place_ref[0], low * 2.0**-20, high * 2.0**-20)


def factor_one(halves, starts, ranks, place, x2):
    return pl.pallas_call(
        factor_one_kernel,
        out_shape=(
            jax.ShapeDtypeStruct((R, N), F32),
            jax.ShapeDtypeStruct((4, N, 128), F32),
            HALF,
            HALF,
        ),
        in_specs=[VMEM, VMEM, VMEM, SMEM, SMEM, HBM],
        out_specs=(VMEM,) * 4,
        scratch_shapes=[
            pltpu.VMEM((N, N), BF),
            pltpu.VMEM((N, N), BF),
            pltpu.VMEM((2, 8, N, N), BF),
            pltpu.SemaphoreType.DMA,
        ],
        compiler_params=pltpu.CompilerParams(vmem_limit_bytes=48 * 2**20),
        name="factor_one",
    )(*halves, starts, ranks, place, x2)


def factor_two_kernel(mine_ref, other_ref, start_ref, rank_ref, place_ref, a_ref, u_ref, y_ref, gh_ref, gl_ref):
    v = masked_factor((mine_ref, other_ref), start_ref, rank_ref, place_ref, 1, gh_ref, gl_ref)
    u_ref[...] = v
    vh, vl = split(v)
    vs = jnp.concatenate([vh, vl], axis=0)
    ah, al = split(jnp.concatenate([a_ref[q] for q in range(4)], axis=1))
    y = mm(ah, vs, NT) + mm(al, vs, NT)
    y = y + pltpu.roll(y, R, 1)
    rolled = [y if k == 0 else pltpu.roll(y, 8 * k, 1) for k in range(8)]
    group = lax.broadcasted_iota(jnp.int32, (8, 128), 1) // 8
    for bx in range(8):
        for by in range(4):
            tile = jnp.zeros((8, 128), F32)
            for r in range(16):
                at = (by * 16 + r) * 8
                tile = jnp.where(group == r, rolled[(r - bx) % 8][at : at + 8, :], tile)
            y_ref[bx * 4 + by] = tile


def factor_two(halves, starts, ranks, place, a):
    return pl.pallas_call(
        factor_two_kernel,
        out_shape=(
            jax.ShapeDtypeStruct((R, N), F32),
            jax.ShapeDtypeStruct((32, 8, 128), F32),
        ),
        in_specs=[VMEM, VMEM, VMEM, SMEM, SMEM, VMEM],
        out_specs=(VMEM, VMEM),
        scratch_shapes=[pltpu.VMEM((N, N), BF), pltpu.VMEM((N, N), BF)],
        compiler_params=pltpu.CompilerParams(vmem_limit_bytes=32 * 2**20),
        name="factor_two",
    )(*halves, starts, ranks, place, a)


def pack_kernel(y_ref, out_ref):
    group = lax.broadcasted_iota(jnp.int32, (32, 128), 1) // 16
    for z in range(8):
        rows = jnp.zeros((32, 128), F32)
        for g in range(8):
            at = 8 * (g % 4) + 4 * (g // 4)
            tile = y_ref[at : at + 4].reshape(32, 128)
            if g != z:
                tile = pltpu.roll(tile, (16 * (g - z)) % 128, 1)
            rows = jnp.where(group == g, tile, rows)
        out_ref[z] = rows


def pack(y):
    return pl.pallas_call(
        pack_kernel,
        out_shape=jax.ShapeDtypeStruct((8, 32, 128), F32),
        in_specs=[VMEM],
        out_specs=VMEM,
        name="pack",
    )(y)


def gram_three_kernel(place_ref, y_ref, keep_ref, send_ref, b_ref):
    lane = lax.broadcasted_iota(jnp.int32, (32, 128), 1)
    for z in range(8):
        y = y_ref[z]
        b_ref[64 * z : 64 * z + 32, :] = jnp.where(lane < R, y, 0.0)
        b_ref[64 * z + 32 : 64 * z + 64, :] = jnp.where(lane < R, pltpu.roll(y, R, 1), 0.0)
    bh, bl = split(b_ref[...])
    low = mm(bh[:256], bh, NT) + mm(bh[:256], bl, NT) + mm(bl[:256], bh, NT)
    high = mm(bh[256:], bh[256:], NT) + mm(bh[256:], bl[256:], NT) + mm(bl[256:], bh[256:], NT)
    put_blocks(keep_ref, send_ref, place_ref[0], low * 2.0**-20, high * 2.0**-20)


def gram_three(place, y):
    return pl.pallas_call(
        gram_three_kernel,
        out_shape=(HALF, HALF, jax.ShapeDtypeStruct((N, 128), F32)),
        in_specs=[SMEM, VMEM],
        out_specs=(VMEM, VMEM, VMEM),
        compiler_params=pltpu.CompilerParams(vmem_limit_bytes=32 * 2**20),
        name="gram_three",
    )(place, y)


def factor_three_kernel(
    mine_ref, other_ref, start_ref, rank_ref, place_ref, b_ref, u_one_ref, u_two_ref, u_ref, core_ref, gh_ref, gl_ref
):
    v = masked_factor((mine_ref, other_ref), start_ref, rank_ref, place_ref, 2, gh_ref, gl_ref)
    u_ref[0] = u_one_ref[...]
    u_ref[1] = u_two_ref[...]
    u_ref[2] = v
    vh, vl = split(v)
    bh, bl = split(b_ref[...])
    t = mm(jnp.concatenate([vh, vl], axis=0), bh)
    core = t[:R] + t[R:] + mm(vh, bl)
    core = jnp.concatenate([core, core], axis=0).T
    for s in range(4):
        for e in range(2):
            core_ref[s, e] = core[16 * s + 8 * e : 16 * s + 8 * e + 8, :R]


def factor_three(halves, starts, ranks, place, b, u_one, u_two):
    return pl.pallas_call(
        factor_three_kernel,
        out_shape=(
            jax.ShapeDtypeStruct((3, R, N), F32),
            jax.ShapeDtypeStruct((4, 2, 8, R), F32),
        ),
        in_specs=[VMEM, VMEM, VMEM, SMEM, SMEM, VMEM, VMEM, VMEM],
        out_specs=(VMEM, VMEM),
        scratch_shapes=[pltpu.VMEM((N, N), BF), pltpu.VMEM((N, N), BF)],
        compiler_params=pltpu.CompilerParams(vmem_limit_bytes=32 * 2**20),
        name="factor_three",
    )(*halves, starts, ranks, place, b, u_one, u_two)


PLANE = ("y", "gy")


def swap(x, axes):
    return lax.all_to_all(x, axes, 0, 0, tiled=True)


def spread(x, axes, count):
    return swap(jnp.broadcast_to(x[None], (count,) + x.shape), axes)


def other_core(x):
    return lax.ppermute(x, "core", [(0, 1), (1, 0)])


def total(keep, send):
    g = keep + other_core(send)
    g = jnp.sum(swap(g.reshape(16, 40, 128), PLANE), axis=0)
    g = jnp.sum(spread(g, "gz", 8), axis=0)
    g = spread(g, PLANE, 16).reshape(5, 128, 128)
    return g, other_core(g)


def local(tensor, starts, trunc_ranks):
    starts_t = jnp.swapaxes(starts, 1, 2)
    place = lax.axis_index("core").astype(jnp.int32).reshape(1)
    tensor, place = lax.optimization_barrier((tensor, place))
    x = tensor.reshape(4, 64, 8, 8, 128).transpose(0, 2, 1, 3, 4).reshape(32, N, 128)
    x = swap(x, ("y", "core", "gy")).reshape(8, 4, N, 128)
    keep, send, x2 = gram_one(place, x)
    u_one, a, keep, send = factor_one(total(keep, send), starts_t, trunc_ranks, place, x2)
    u_two, y = factor_two(total(keep, send), starts_t, trunc_ranks, place, a)
    y = pack(swap(y, ("y", "core", "gy")))
    keep, send, b = gram_three(place, swap(y, "gz"))
    factors, core_out = factor_three(total(keep, send), starts_t, trunc_ranks, place, b, u_one, u_two)
    return (jnp.swapaxes(core_out, 2, 3), jnp.swapaxes(factors, 1, 2))


def solution(mesh):
    fine = jax.sharding.Mesh(mesh.devices.reshape(4, 2, 4, 8), ("y", "core", "gy", "gz"))
    gx = ("y", "core")
    return jax.shard_map(
        local,
        mesh=fine,
        in_specs=(P(None, gx, "gz", "gy"), P(), P()),
        out_specs=(P(None, ("gy", "gz"), None, gx), P()),
        check_vma=False,
    )
```

```python
import jax
import jax.numpy as jnp
from jax import lax
from jax.experimental import pallas as pl
from jax.experimental.pallas import tpu as pltpu
from jax.sharding import PartitionSpec as P

N = 512
R = 64
ITERS = 4
BF = jnp.bfloat16
F32 = jnp.float32
PAIRS = [(a, b) for a in range(4) for b in range(a, 4)]
NT = (((1,), (1,)), ((), ()))
NN = (((1,), (0,)), ((), ()))
VMEM = pl.BlockSpec(memory_space=pltpu.VMEM)
SMEM = pl.BlockSpec(memory_space=pltpu.SMEM)
HBM = pl.BlockSpec(memory_space=pltpu.HBM)


def split(x):
    hi = x.astype(BF)
    return hi, (x - hi.astype(F32)).astype(BF)


def mm(a, b, dims=NN):
    return lax.dot_general(a, b, dims, preferred_element_type=F32)


def put_blocks(keep_ref, send_ref, core, low, high):
    for here in range(2):

        @pl.when(core == here)
        def _():
            for n, (a, b) in enumerate(PAIRS):
                out_ref = keep_ref if n // 5 == here else send_ref
                if a < 2:
                    out_ref[n % 5] = low[a * 128 : a * 128 + 128, b * 128 : b * 128 + 128]
                else:
                    out_ref[n % 5] = high[a * 128 - 256 : a * 128 - 128, b * 128 - 256 : b * 128 - 128]


HALF = jax.ShapeDtypeStruct((5, 128, 128), F32)


def column(x, j):
    return jnp.broadcast_to(x[:, R + j : R + j + 1], (8, 128))


def row(x, k):
    return jnp.broadcast_to(x[k : k + 1, :], (8, 128))


def inverse_factor(cc):
    row8 = lax.broadcasted_iota(jnp.int32, (8, 128), 0)
    lane = lax.broadcasted_iota(jnp.int32, (8, 128), 1)
    m = [
        jnp.where(lane < R, (lane == row8 + 8 * b).astype(F32), cc[8 * b : 8 * b + 8, :])
        for b in range(8)
    ]
    scale = []
    diag = [column(m[0], k) for k in range(8)]
    for b0 in range(8):
        below = [[column(m[b], 8 * b0 + k) for b in range(b0 + 1, 8)] for k in range(8)]
        ahead = [column(m[b0 + 1], 8 * b0 + 8 + k) for k in range(8)] if b0 < 7 else []
        pivots = jnp.ones((8, 128), F32)
        for k in range(8):
            pivot = row(diag[k], k)
            inv = 1.0 / pivot
            scaled_row = row(m[b0], k) * inv
            rest = jnp.where(row8 > k, diag[k], 0.0)
            pivots = jnp.where(row8 == k, pivot, pivots)
            factors = {k2: row(diag[k2], k) * inv for k2 in range(k + 1, 8)}
            for k2 in factors:
                diag[k2] = diag[k2] - rest * factors[k2]
            m[b0] = m[b0] - rest * scaled_row
            for n in range(7 - b0):
                m[b0 + 1 + n] = m[b0 + 1 + n] - below[k][n] * scaled_row
                for k2 in factors:
                    below[k2][n] = below[k2][n] - below[k][n] * factors[k2]
            for k2 in range(len(ahead)):
                ahead[k2] = ahead[k2] - below[k][0] * (row(below[k][0], k2) * inv)
        scale.append(pivots)
        diag = ahead
    out = []
    for b in range(8):
        y = lax.rsqrt(scale[b])
        y = y * (1.5 - 0.5 * (scale[b] * y) * y)
        out.append(m[b] * y)
    return jnp.concatenate(out, axis=0)


def subspace(halves, core, start, gh_ref, gl_ref):
    for here in range(2):

        @pl.when(core == here)
        def _():
            for n, (a, b) in enumerate(PAIRS):
                blk = halves[(n // 5 + here) % 2][n % 5]
                hi, lo = split(blk)
                gh_ref[a * 128 : a * 128 + 128, b * 128 : b * 128 + 128] = hi
                gl_ref[a * 128 : a * 128 + 128, b * 128 : b * 128 + 128] = lo
                if a != b:
                    hi, lo = split(blk.T)
                    gh_ref[b * 128 : b * 128 + 128, a * 128 : a * 128 + 128] = hi
                    gl_ref[b * 128 : b * 128 + 128, a * 128 : a * 128 + 128] = lo

    lane = lax.broadcasted_iota(jnp.int32, (R, 128), 1)

    def image(vh, vs):
        t = mm(vs, gh_ref[...])
        return t[:R] + t[R:] + mm(vh, gl_ref[...])

    def step(k, w):
        wh, wl = split(w)
        ws = jnp.concatenate([wh, wl], axis=0)
        c = mm(ws, ws, NT)
        c = c[:R] + c[R:]
        z = jnp.where(k == ITERS - 1, w, image(wh, ws))
        zh, zl = split(z)
        li = inverse_factor(c + pltpu.roll(c, R, 1))
        lh = li.astype(BF).astype(F32)
        both = jnp.where(lane < R, lh, pltpu.roll(li - lh, R, 1)).astype(BF)
        return mm(
            jnp.concatenate([both, both], axis=1),
            jnp.concatenate([zh, zh, zl, zl], axis=0),
        )

    vh, vl = split(start)
    return lax.fori_loop(0, ITERS, step, image(vh, jnp.concatenate([vh, vl], axis=0)))


def masked_factor(halves, start_ref, rank_ref, place_ref, mode, gh_ref, gl_ref):
    v = subspace(halves, place_ref[0], start_ref[mode], gh_ref, gl_ref)
    index = lax.broadcasted_iota(jnp.int32, (R, N), 0)
    return jnp.where(index < rank_ref[mode], v, 0.0)


def gram_one_kernel(place_ref, x_ref, keep_ref, send_ref, x2_ref, low_ref, high_ref, cross_ref):
    step = pl.program_id(0)

    @pl.when(step == 0)
    def _():
        low_ref[...] = jnp.zeros_like(low_ref)
        high_ref[...] = jnp.zeros_like(high_ref)
        cross_ref[...] = jnp.zeros_like(cross_ref)

    for p in range(8):
        for g in range(8):
            hi, lo = split(x_ref[g, 0, pl.ds(p, 64, stride=8), :])
            x2_ref[0, p, g * 64 : g * 64 + 64, :] = hi
            x2_ref[1, p, g * 64 : g * 64 + 64, :] = lo
    for p in range(0, 8, 4):
        xh = jnp.concatenate([x2_ref[0, p + k] for k in range(4)], axis=1)
        xl = jnp.concatenate([x2_ref[1, p + k] for k in range(4)], axis=1)
        low_ref[...] += mm(xh[:256], xh, NT)
        high_ref[...] += mm(xh[256:], xh[256:], NT)
        cross_ref[...] += mm(xh, xl, NT)

    @pl.when(step == pl.num_programs(0) - 1)
    def _():
        cross = cross_ref[...]
        cross = cross + cross.T
        low = low_ref[...] + cross[:256]
        high = high_ref[...] + cross[256:, 256:]
        put_blocks(keep_ref, send_ref, place_ref[0], low * 2.0**-20, high * 2.0**-20)


def gram_one(place, x):
    half = pl.BlockSpec((5, 128, 128), lambda i: (0, 0, 0))
    return pl.pallas_call(
        gram_one_kernel,
        grid=(4,),
        out_shape=(HALF, HALF, pltpu.HBM((2, 8, N, N), BF)),
        in_specs=[SMEM, pl.BlockSpec((8, 1, N, 128), lambda i: (0, i, 0, 0))],
        out_specs=(half, half, pl.BlockSpec((2, 8, N, 128), lambda i: (0, 0, 0, i))),
        scratch_shapes=[pltpu.VMEM((256, N), F32), pltpu.VMEM((256, 256), F32), pltpu.VMEM((N, N), F32)],
        compiler_params=pltpu.CompilerParams(vmem_limit_bytes=40 * 2**20),
        name="gram_one",
    )(place, x)


def factor_one_kernel(
    mine_ref, other_ref, start_ref, rank_ref, place_ref, x_hbm, u_ref, a_ref, keep_ref, send_ref, gh_ref, gl_ref, x_ref, sem
):
    copy = pltpu.make_async_copy(x_hbm, x_ref, sem)
    copy.start()
    v = masked_factor((mine_ref, other_ref), start_ref, rank_ref, place_ref, 0, gh_ref, gl_ref)
    u_ref[...] = v
    vh, vl = split(v)
    vs = jnp.concatenate([vh, vl], axis=0)
    copy.wait()
    for p in range(8):
        t = mm(vs, x_ref[0, p])
        y = t[:R] + t[R:] + mm(vh, x_ref[1, p])
        for q in range(4):
            a_ref[q, pl.ds(p, R, stride=8), :] = y[:, 128 * q : 128 * q + 128]
    a = jnp.concatenate([a_ref[q] for q in range(4)], axis=1)
    ah, al = split(a)
    th, tl = split(a.T)
    low = mm(th[:256], ah) + mm(th[:256], al) + mm(tl[:256], ah)
    high = mm(th[256:], ah[:, 256:]) + mm(th[256:], al[:, 256:]) + mm(tl[256:], ah[:, 256:])
    put_blocks(keep_ref, send_ref, place_ref[0], low * 2.0**-20, high * 2.0**-20)


def factor_one(halves, starts, ranks, place, x2):
    return pl.pallas_call(
        factor_one_kernel,
        out_shape=(
            jax.ShapeDtypeStruct((R, N), F32),
            jax.ShapeDtypeStruct((4, N, 128), F32),
            HALF,
            HALF,
        ),
        in_specs=[VMEM, VMEM, VMEM, SMEM, SMEM, HBM],
        out_specs=(VMEM,) * 4,
        scratch_shapes=[
            pltpu.VMEM((N, N), BF),
            pltpu.VMEM((N, N), BF),
            pltpu.VMEM((2, 8, N, N), BF),
            pltpu.SemaphoreType.DMA,
        ],
        compiler_params=pltpu.CompilerParams(vmem_limit_bytes=48 * 2**20),
        name="factor_one",
    )(*halves, starts, ranks, place, x2)


def factor_two_kernel(
    mine_ref, other_ref, start_ref, rank_ref, place_ref, a_ref, u_ref, out_ref, gh_ref, gl_ref, y_ref
):
    v = masked_factor((mine_ref, other_ref), start_ref, rank_ref, place_ref, 1, gh_ref, gl_ref)
    u_ref[...] = v
    vh, vl = split(v)
    vs = jnp.concatenate([vh, vl], axis=0)
    ah, al = split(jnp.concatenate([a_ref[q] for q in range(4)], axis=1))
    y = mm(ah, vs, NT) + mm(al, vs, NT)
    y_ref[...] = y + pltpu.roll(y, R, 1)
    group = lax.broadcasted_iota(jnp.int32, (8, 128), 1) // 8
    for by in range(4):
        tiles = [jnp.zeros((8, 128), F32) for _ in range(8)]
        for p in range(8):
            for e in range(2):
                rows = y_ref[pl.ds(by * 128 + e * 8 + p, 8, stride=16), :]
                for bx in range(8):
                    shift = (2 * p + e - bx) % 8
                    moved = pltpu.roll(rows, 8 * shift, 1) if shift else rows
                    tiles[bx] = jnp.where(group == 2 * p + e, moved, tiles[bx])
        for bx in range(8):
            out_ref[bx * 32 + by * 8 : bx * 32 + by * 8 + 8, :] = tiles[bx]


def factor_two(halves, starts, ranks, place, a):
    return pl.pallas_call(
        factor_two_kernel,
        out_shape=(
            jax.ShapeDtypeStruct((R, N), F32),
            jax.ShapeDtypeStruct((256, 128), F32),
        ),
        in_specs=[VMEM, VMEM, VMEM, SMEM, SMEM, VMEM],
        out_specs=(VMEM, VMEM),
        scratch_shapes=[pltpu.VMEM((N, N), BF), pltpu.VMEM((N, N), BF), pltpu.VMEM((N, 128), F32)],
        compiler_params=pltpu.CompilerParams(vmem_limit_bytes=32 * 2**20),
        name="factor_two",
    )(*halves, starts, ranks, place, a)


def gram_three_kernel(place_ref, y_ref, keep_ref, send_ref, b_ref):
    group = lax.broadcasted_iota(jnp.int32, (8, 128), 1) // 16
    for pg in range(8):
        for p in range(8):
            rows = jnp.zeros((8, 128), F32)
            for s in range(4):
                at = (8 * s + pg) * 8
                tile = y_ref[at : at + 8, :]
                if s != p:
                    tile = pltpu.roll(tile, (16 * (s - p)) % 128, 1)
                rows = jnp.where(group == s, tile, rows)
            b_ref[pl.ds(8 * pg + p, 8, stride=R), :] = rows
    bh, bl = split(b_ref[...])
    low = mm(bh[:256], bh, NT) + mm(bh[:256], bl, NT) + mm(bl[:256], bh, NT)
    high = mm(bh[256:], bh[256:], NT) + mm(bh[256:], bl[256:], NT) + mm(bl[256:], bh[256:], NT)
    put_blocks(keep_ref, send_ref, place_ref[0], low * 2.0**-20, high * 2.0**-20)


def gram_three(place, y):
    return pl.pallas_call(
        gram_three_kernel,
        out_shape=(HALF, HALF, jax.ShapeDtypeStruct((N, 128), F32)),
        in_specs=[SMEM, VMEM],
        out_specs=(VMEM, VMEM, VMEM),
        compiler_params=pltpu.CompilerParams(vmem_limit_bytes=32 * 2**20),
        name="gram_three",
    )(place, y)


def factor_three_kernel(
    mine_ref, other_ref, start_ref, rank_ref, place_ref, b_ref, u_one_ref, u_two_ref, u_ref, core_ref, gh_ref, gl_ref
):
    v = masked_factor((mine_ref, other_ref), start_ref, rank_ref, place_ref, 2, gh_ref, gl_ref)
    u_ref[0] = u_one_ref[...]
    u_ref[1] = u_two_ref[...]
    u_ref[2] = v
    vh, vl = split(v)
    bh, bl = split(b_ref[...])
    t = mm(jnp.concatenate([vh, vl], axis=0), bh)
    core = t[:R] + t[R:] + mm(vh, bl)
    core = jnp.concatenate([core, core], axis=0).T
    for s in range(4):
        for e in range(2):
            core_ref[s, e] = core[16 * s + 8 * e : 16 * s + 8 * e + 8, :R]


def factor_three(halves, starts, ranks, place, b, u_one, u_two):
    return pl.pallas_call(
        factor_three_kernel,
        out_shape=(
            jax.ShapeDtypeStruct((3, R, N), F32),
            jax.ShapeDtypeStruct((4, 2, 8, R), F32),
        ),
        in_specs=[VMEM, VMEM, VMEM, SMEM, SMEM, VMEM, VMEM, VMEM],
        out_specs=(VMEM, VMEM),
        scratch_shapes=[pltpu.VMEM((N, N), BF), pltpu.VMEM((N, N), BF)],
        compiler_params=pltpu.CompilerParams(vmem_limit_bytes=32 * 2**20),
        name="factor_three",
    )(*halves, starts, ranks, place, b, u_one, u_two)


PLANE = ("y", "gy")


def swap(x, axes):
    return lax.all_to_all(x, axes, 0, 0, tiled=True)


def spread(x, axes, count):
    return swap(jnp.broadcast_to(x[None], (count,) + x.shape), axes)


def other_core(x):
    return lax.ppermute(x, "core", [(0, 1), (1, 0)])


def total(keep, send):
    g = keep + other_core(send)
    g = jnp.sum(swap(g.reshape(16, 40, 128), PLANE), axis=0)
    g = jnp.sum(spread(g, "gz", 8), axis=0)
    g = spread(g, PLANE, 16).reshape(5, 128, 128)
    return g, other_core(g)


def local(tensor, starts, trunc_ranks):
    starts_t = jnp.swapaxes(starts, 1, 2)
    place = lax.axis_index("core").astype(jnp.int32).reshape(1)
    tensor, place = lax.optimization_barrier((tensor, place))
    x = tensor.reshape(4, 64, 8, 8, 128).transpose(0, 2, 1, 3, 4).reshape(32, N, 128)
    x = swap(x, ("y", "core", "gy")).reshape(8, 4, N, 128)
    keep, send, x2 = gram_one(place, x)
    u_one, a, keep, send = factor_one(total(keep, send), starts_t, trunc_ranks, place, x2)
    u_two, y = factor_two(total(keep, send), starts_t, trunc_ranks, place, a)
    y = swap(y.reshape(256, 1, 128), ("y", "core", "gy", "gz")).reshape(256, 128)
    keep, send, b = gram_three(place, y)
    factors, core_out = factor_three(total(keep, send), starts_t, trunc_ranks, place, b, u_one, u_two)
    return (jnp.swapaxes(core_out, 2, 3), jnp.swapaxes(factors, 1, 2))


def solution(mesh):
    fine = jax.sharding.Mesh(mesh.devices.reshape(4, 2, 4, 8), ("y", "core", "gy", "gz"))
    gx = ("y", "core")
    return jax.shard_map(
        local,
        mesh=fine,
        in_specs=(P(None, gx, "gz", "gy"), P(), P()),
        out_specs=(P(None, ("gy", "gz"), None, gx), P()),
        check_vma=False,
    )
```

```python
import jax
import jax.numpy as jnp
from jax import lax
from jax.experimental import pallas as pl
from jax.experimental.pallas import tpu as pltpu
from jax.sharding import PartitionSpec as P

N = 512
R = 64
ITERS = 4
BF = jnp.bfloat16
F32 = jnp.float32
PAIRS = [(a, b) for a in range(4) for b in range(a, 4)]
NT = (((1,), (1,)), ((), ()))
NN = (((1,), (0,)), ((), ()))
VMEM = pl.BlockSpec(memory_space=pltpu.VMEM)
SMEM = pl.BlockSpec(memory_space=pltpu.SMEM)
HBM = pl.BlockSpec(memory_space=pltpu.HBM)


def split(x):
    hi = x.astype(BF)
    return hi, (x - hi.astype(F32)).astype(BF)


def mm(a, b, dims=NN):
    return lax.dot_general(a, b, dims, preferred_element_type=F32)


def put_blocks(keep_ref, send_ref, core, low, high):
    for here in range(2):

        @pl.when(core == here)
        def _():
            for n, (a, b) in enumerate(PAIRS):
                out_ref = keep_ref if n // 5 == here else send_ref
                if a < 2:
                    out_ref[n % 5] = low[a * 128 : a * 128 + 128, b * 128 : b * 128 + 128]
                else:
                    out_ref[n % 5] = high[a * 128 - 256 : a * 128 - 128, b * 128 - 256 : b * 128 - 128]


HALF = jax.ShapeDtypeStruct((5, 128, 128), F32)


def column(x, j):
    return jnp.broadcast_to(x[:, R + j : R + j + 1], (8, 128))


def row(x, k):
    return jnp.broadcast_to(x[k : k + 1, :], (8, 128))


def inverse_factor(cc):
    row8 = lax.broadcasted_iota(jnp.int32, (8, 128), 0)
    lane = lax.broadcasted_iota(jnp.int32, (8, 128), 1)
    m = [
        jnp.where(lane < R, (lane == row8 + 8 * b).astype(F32), cc[8 * b : 8 * b + 8, :])
        for b in range(8)
    ]
    scale = []
    diag = [column(m[0], k) for k in range(8)]
    for b0 in range(8):
        below = [[column(m[b], 8 * b0 + k) for b in range(b0 + 1, 8)] for k in range(8)]
        ahead = [column(m[b0 + 1], 8 * b0 + 8 + k) for k in range(8)] if b0 < 7 else []
        pivots = jnp.ones((8, 128), F32)
        for k in range(8):
            pivot = row(diag[k], k)
            inv = 1.0 / pivot
            rest = jnp.where(row8 > k, diag[k], 0.0) * inv
            pivots = jnp.where(row8 == k, pivot, pivots)
            pivot_row = row(m[b0], k)
            heads = {k2: row(diag[k2], k) for k2 in range(k + 1, 8)}
            for k2 in heads:
                diag[k2] = diag[k2] - rest * heads[k2]
            m[b0] = m[b0] - rest * pivot_row
            for n in range(7 - b0):
                ratio = below[k][n] * inv
                m[b0 + 1 + n] = m[b0 + 1 + n] - ratio * pivot_row
                for k2 in heads:
                    below[k2][n] = below[k2][n] - ratio * heads[k2]
                if n == 0:
                    for k2 in range(8):
                        ahead[k2] = ahead[k2] - below[k][0] * row(ratio, k2)
        scale.append(pivots)
        diag = ahead
    out = []
    for b in range(8):
        y = lax.rsqrt(scale[b])
        y = y * (1.5 - 0.5 * (scale[b] * y) * y)
        out.append(m[b] * y)
    return jnp.concatenate(out, axis=0)


def subspace(halves, core, start, gh_ref, gl_ref):
    for here in range(2):

        @pl.when(core == here)
        def _():
            for n, (a, b) in enumerate(PAIRS):
                blk = halves[(n // 5 + here) % 2][n % 5]
                hi, lo = split(blk)
                gh_ref[a * 128 : a * 128 + 128, b * 128 : b * 128 + 128] = hi
                gl_ref[a * 128 : a * 128 + 128, b * 128 : b * 128 + 128] = lo
                if a != b:
                    hi, lo = split(blk.T)
                    gh_ref[b * 128 : b * 128 + 128, a * 128 : a * 128 + 128] = hi
                    gl_ref[b * 128 : b * 128 + 128, a * 128 : a * 128 + 128] = lo

    lane = lax.broadcasted_iota(jnp.int32, (R, 128), 1)

    def image(vh, vs):
        t = mm(vs, gh_ref[...])
        return t[:R] + t[R:] + mm(vh, gl_ref[...])

    def step(k, w):
        wh, wl = split(w)
        ws = jnp.concatenate([wh, wl], axis=0)
        c = mm(ws, ws, NT)
        c = c[:R] + c[R:]
        z = jnp.where(k == ITERS - 1, w, image(wh, ws))
        zh, zl = split(z)
        li = inverse_factor(c + pltpu.roll(c, R, 1))
        lh = li.astype(BF).astype(F32)
        both = jnp.where(lane < R, lh, pltpu.roll(li - lh, R, 1)).astype(BF)
        return mm(
            jnp.concatenate([both, both], axis=1),
            jnp.concatenate([zh, zh, zl, zl], axis=0),
        )

    vh, vl = split(start)
    return lax.fori_loop(0, ITERS, step, image(vh, jnp.concatenate([vh, vl], axis=0)))


def masked_factor(halves, start_ref, rank_ref, place_ref, mode, gh_ref, gl_ref):
    v = subspace(halves, place_ref[0], start_ref[mode], gh_ref, gl_ref)
    index = lax.broadcasted_iota(jnp.int32, (R, N), 0)
    return jnp.where(index < rank_ref[mode], v, 0.0)


def regroup_kernel(x_hbm, out_ref, sem):
    copies = [
        pltpu.make_async_copy(x_hbm.at[s, :, pl.ds(8 * g, 8), :], out_ref.at[8 * s + g], sem.at[8 * s + g])
        for s in range(4)
        for g in range(8)
    ]
    for c in copies:
        c.start()
    for c in copies:
        c.wait()


def regroup(x):
    return pl.pallas_call(
        regroup_kernel,
        out_shape=jax.ShapeDtypeStruct((32, 64, 8, 128), F32),
        in_specs=[HBM],
        out_specs=VMEM,
        scratch_shapes=[pltpu.SemaphoreType.DMA((32,))],
        compiler_params=pltpu.CompilerParams(vmem_limit_bytes=42 * 2**20),
        name="regroup",
    )(x)


def gram_one_kernel(place_ref, x_ref, keep_ref, send_ref, x2_ref, low_ref, high_ref, cross_ref):
    step = pl.program_id(0)

    @pl.when(step == 0)
    def _():
        low_ref[...] = jnp.zeros_like(low_ref)
        high_ref[...] = jnp.zeros_like(high_ref)
        cross_ref[...] = jnp.zeros_like(cross_ref)

    for p in range(0, 8, 2):
        his, los = [], []
        for k in (p, p + 1):
            parts = [split(x_ref[g, 0, pl.ds(k, 64, stride=8), :]) for g in range(8)]
            hi = jnp.concatenate([h for h, _ in parts], axis=0)
            lo = jnp.concatenate([l for _, l in parts], axis=0)
            x2_ref[0, k] = hi
            x2_ref[1, k] = lo
            his.append(hi)
            los.append(lo)
        xh = jnp.concatenate(his, axis=1)
        low_ref[...] += mm(xh[:256], xh, NT)
        high_ref[...] += mm(xh[256:], xh[256:], NT)
        cross_ref[...] += mm(xh, jnp.concatenate(los, axis=1), NT)

    @pl.when(step == pl.num_programs(0) - 1)
    def _():
        cross = cross_ref[...]
        cross = cross + cross.T
        low = low_ref[...] + cross[:256]
        high = high_ref[...] + cross[256:, 256:]
        put_blocks(keep_ref, send_ref, place_ref[0], low * 2.0**-20, high * 2.0**-20)


def gram_one(place, x):
    half = pl.BlockSpec((5, 128, 128), lambda i: (0, 0, 0))
    return pl.pallas_call(
        gram_one_kernel,
        grid=(4,),
        out_shape=(HALF, HALF, pltpu.HBM((2, 8, N, N), BF)),
        in_specs=[SMEM, pl.BlockSpec((8, 1, N, 128), lambda i: (0, i, 0, 0))],
        out_specs=(half, half, pl.BlockSpec((2, 8, N, 128), lambda i: (0, 0, 0, i))),
        scratch_shapes=[pltpu.VMEM((256, N), F32), pltpu.VMEM((256, 256), F32), pltpu.VMEM((N, N), F32)],
        compiler_params=pltpu.CompilerParams(vmem_limit_bytes=40 * 2**20),
        name="gram_one",
    )(place, x)


def factor_one_kernel(
    mine_ref, other_ref, start_ref, rank_ref, place_ref, x_hbm, u_ref, a_ref, keep_ref, send_ref, gh_ref, gl_ref, x_ref, sem
):
    copy = pltpu.make_async_copy(x_hbm, x_ref, sem)
    copy.start()
    v = masked_factor((mine_ref, other_ref), start_ref, rank_ref, place_ref, 0, gh_ref, gl_ref)
    u_ref[...] = v
    vh, vl = split(v)
    vs = jnp.concatenate([vh, vl], axis=0)
    copy.wait()
    for p in range(8):
        t = mm(vs, x_ref[0, p])
        y = t[:R] + t[R:] + mm(vh, x_ref[1, p])
        for q in range(4):
            a_ref[q, pl.ds(p, R, stride=8), :] = y[:, 128 * q : 128 * q + 128]
    a = jnp.concatenate([a_ref[q] for q in range(4)], axis=1)
    ah, al = split(a)
    th, tl = split(a.T)
    low = mm(th[:256], ah) + mm(th[:256], al) + mm(tl[:256], ah)
    high = mm(th[256:], ah[:, 256:]) + mm(th[256:], al[:, 256:]) + mm(tl[256:], ah[:, 256:])
    put_blocks(keep_ref, send_ref, place_ref[0], low * 2.0**-20, high * 2.0**-20)


def factor_one(halves, starts, ranks, place, x2):
    return pl.pallas_call(
        factor_one_kernel,
        out_shape=(
            jax.ShapeDtypeStruct((R, N), F32),
            jax.ShapeDtypeStruct((4, N, 128), F32),
            HALF,
            HALF,
        ),
        in_specs=[VMEM, VMEM, VMEM, SMEM, SMEM, HBM],
        out_specs=(VMEM,) * 4,
        scratch_shapes=[
            pltpu.VMEM((N, N), BF),
            pltpu.VMEM((N, N), BF),
            pltpu.VMEM((2, 8, N, N), BF),
            pltpu.SemaphoreType.DMA,
        ],
        compiler_params=pltpu.CompilerParams(vmem_limit_bytes=48 * 2**20),
        name="factor_one",
    )(*halves, starts, ranks, place, x2)


def factor_two_kernel(
    mine_ref, other_ref, start_ref, rank_ref, place_ref, a_ref, u_ref, out_ref, gh_ref, gl_ref, y_ref
):
    v = masked_factor((mine_ref, other_ref), start_ref, rank_ref, place_ref, 1, gh_ref, gl_ref)
    u_ref[...] = v
    vh, vl = split(v)
    vs = jnp.concatenate([vh, vl], axis=0)
    ah, al = split(jnp.concatenate([a_ref[q] for q in range(4)], axis=1))
    y = mm(ah, vs, NT) + mm(al, vs, NT)
    y_ref[...] = y + pltpu.roll(y, R, 1)
    group = lax.broadcasted_iota(jnp.int32, (8, 128), 1) // 8
    for by in range(4):
        tiles = [jnp.zeros((8, 128), F32) for _ in range(8)]
        for p in range(8):
            for e in range(2):
                rows = y_ref[pl.ds(by * 128 + e * 8 + p, 8, stride=16), :]
                for bx in range(8):
                    shift = (2 * p + e - bx) % 8
                    moved = pltpu.roll(rows, 8 * shift, 1) if shift else rows
                    tiles[bx] = jnp.where(group == 2 * p + e, moved, tiles[bx])
        for bx in range(8):
            out_ref[bx * 32 + by * 8 : bx * 32 + by * 8 + 8, :] = tiles[bx]


def factor_two(halves, starts, ranks, place, a):
    return pl.pallas_call(
        factor_two_kernel,
        out_shape=(
            jax.ShapeDtypeStruct((R, N), F32),
            jax.ShapeDtypeStruct((256, 128), F32),
        ),
        in_specs=[VMEM, VMEM, VMEM, SMEM, SMEM, VMEM],
        out_specs=(VMEM, VMEM),
        scratch_shapes=[pltpu.VMEM((N, N), BF), pltpu.VMEM((N, N), BF), pltpu.VMEM((N, 128), F32)],
        compiler_params=pltpu.CompilerParams(vmem_limit_bytes=32 * 2**20),
        name="factor_two",
    )(*halves, starts, ranks, place, a)


def gram_three_kernel(place_ref, y_ref, keep_ref, send_ref, b_ref):
    group = lax.broadcasted_iota(jnp.int32, (8, 128), 1) // 16
    for pg in range(8):
        for p in range(8):
            rows = jnp.zeros((8, 128), F32)
            for s in range(4):
                at = (8 * s + pg) * 8
                tile = y_ref[at : at + 8, :]
                if s != p:
                    tile = pltpu.roll(tile, (16 * (s - p)) % 128, 1)
                rows = jnp.where(group == s, tile, rows)
            b_ref[pl.ds(8 * pg + p, 8, stride=R), :] = rows
    bh, bl = split(b_ref[...])
    low = mm(bh[:256], bh, NT) + mm(bh[:256], bl, NT) + mm(bl[:256], bh, NT)
    high = mm(bh[256:], bh[256:], NT) + mm(bh[256:], bl[256:], NT) + mm(bl[256:], bh[256:], NT)
    put_blocks(keep_ref, send_ref, place_ref[0], low * 2.0**-20, high * 2.0**-20)


def gram_three(place, y):
    return pl.pallas_call(
        gram_three_kernel,
        out_shape=(HALF, HALF, jax.ShapeDtypeStruct((N, 128), F32)),
        in_specs=[SMEM, VMEM],
        out_specs=(VMEM, VMEM, VMEM),
        compiler_params=pltpu.CompilerParams(vmem_limit_bytes=32 * 2**20),
        name="gram_three",
    )(place, y)


def factor_three_kernel(
    mine_ref, other_ref, start_ref, rank_ref, place_ref, b_ref, u_one_ref, u_two_ref, u_ref, core_ref, gh_ref, gl_ref
):
    v = masked_factor((mine_ref, other_ref), start_ref, rank_ref, place_ref, 2, gh_ref, gl_ref)
    u_ref[0] = u_one_ref[...]
    u_ref[1] = u_two_ref[...]
    u_ref[2] = v
    vh, vl = split(v)
    bh, bl = split(b_ref[...])
    t = mm(jnp.concatenate([vh, vl], axis=0), bh)
    core = t[:R] + t[R:] + mm(vh, bl)
    core = jnp.concatenate([core, core], axis=0).T
    for s in range(4):
        for e in range(2):
            core_ref[s, e] = core[16 * s + 8 * e : 16 * s + 8 * e + 8, :R]


def factor_three(halves, starts, ranks, place, b, u_one, u_two):
    return pl.pallas_call(
        factor_three_kernel,
        out_shape=(
            jax.ShapeDtypeStruct((3, R, N), F32),
            jax.ShapeDtypeStruct((4, 2, 8, R), F32),
        ),
        in_specs=[VMEM, VMEM, VMEM, SMEM, SMEM, VMEM, VMEM, VMEM],
        out_specs=(VMEM, VMEM),
        scratch_shapes=[pltpu.VMEM((N, N), BF), pltpu.VMEM((N, N), BF)],
        compiler_params=pltpu.CompilerParams(vmem_limit_bytes=32 * 2**20),
        name="factor_three",
    )(*halves, starts, ranks, place, b, u_one, u_two)


PLANE = ("y", "gy")


def swap(x, axes):
    return lax.all_to_all(x, axes, 0, 0, tiled=True)


def spread(x, axes, count):
    return swap(jnp.broadcast_to(x[None], (count,) + x.shape), axes)


def other_core(x):
    return lax.ppermute(x, "core", [(0, 1), (1, 0)])


def total(keep, send):
    g = keep + other_core(send)
    g = jnp.sum(swap(g.reshape(16, 40, 128), PLANE), axis=0)
    g = jnp.sum(spread(g, "gz", 8), axis=0)
    g = spread(g, PLANE, 16).reshape(5, 128, 128)
    return g, other_core(g)


def local(tensor, starts, trunc_ranks):
    starts_t = jnp.swapaxes(starts, 1, 2)
    place = lax.axis_index("core").astype(jnp.int32).reshape(1)
    tensor, place = lax.optimization_barrier((tensor, place))
    x = regroup(tensor).reshape(32, N, 128)
    x = swap(x, ("y", "core", "gy")).reshape(8, 4, N, 128)
    keep, send, x2 = gram_one(place, x)
    u_one, a, keep, send = factor_one(total(keep, send), starts_t, trunc_ranks, place, x2)
    u_two, y = factor_two(total(keep, send), starts_t, trunc_ranks, place, a)
    y = swap(y.reshape(256, 1, 128), ("y", "core", "gy", "gz")).reshape(256, 128)
    keep, send, b = gram_three(place, y)
    factors, core_out = factor_three(total(keep, send), starts_t, trunc_ranks, place, b, u_one, u_two)
    return (jnp.swapaxes(core_out, 2, 3), jnp.swapaxes(factors, 1, 2))


def solution(mesh):
    fine = jax.sharding.Mesh(mesh.devices.reshape(4, 2, 4, 8), ("y", "core", "gy", "gz"))
    gx = ("y", "core")
    return jax.shard_map(
        local,
        mesh=fine,
        in_specs=(P(None, gx, "gz", "gy"), P(), P()),
        out_specs=(P(None, ("gy", "gz"), None, gx), P()),
        check_vma=False,
    )
```

```python
import jax
import jax.numpy as jnp
from jax import lax
from jax.experimental import pallas as pl
from jax.experimental.pallas import tpu as pltpu
from jax.sharding import PartitionSpec as P

N = 512
R = 64
ITERS = 4
BF = jnp.bfloat16
F32 = jnp.float32
PAIRS = [(a, b) for a in range(4) for b in range(a, 4)]
NT = (((1,), (1,)), ((), ()))
NN = (((1,), (0,)), ((), ()))
VMEM = pl.BlockSpec(memory_space=pltpu.VMEM)
SMEM = pl.BlockSpec(memory_space=pltpu.SMEM)
HBM = pl.BlockSpec(memory_space=pltpu.HBM)


def split(x):
    hi = x.astype(BF)
    return hi, (x - hi.astype(F32)).astype(BF)


def split3(x):
    hi = x.astype(BF)
    rest = x - hi.astype(F32)
    mid = rest.astype(BF)
    return hi, mid, (rest - mid.astype(F32)).astype(BF)


def mm(a, b, dims=NN):
    return lax.dot_general(a, b, dims, preferred_element_type=F32)


def put_blocks(keep_ref, send_ref, core, low, high):
    for here in range(2):

        @pl.when(core == here)
        def _():
            for n, (a, b) in enumerate(PAIRS):
                out_ref = keep_ref if n // 5 == here else send_ref
                if a < 2:
                    out_ref[n % 5] = low[a * 128 : a * 128 + 128, b * 128 : b * 128 + 128]
                else:
                    out_ref[n % 5] = high[a * 128 - 256 : a * 128 - 128, b * 128 - 256 : b * 128 - 128]


HALF = jax.ShapeDtypeStruct((5, 128, 128), F32)


def column(x, j):
    return jnp.broadcast_to(x[:, R + j : R + j + 1], (8, 128))


def row(x, k):
    return jnp.broadcast_to(x[k : k + 1, :], (8, 128))


def inverse_factor(cc):
    row8 = lax.broadcasted_iota(jnp.int32, (8, 128), 0)
    lane = lax.broadcasted_iota(jnp.int32, (8, 128), 1)
    m = [
        jnp.where(lane < R, (lane == row8 + 8 * b).astype(F32), cc[8 * b : 8 * b + 8, :])
        for b in range(8)
    ]
    scale = []
    diag = [column(m[0], k) for k in range(8)]
    for b0 in range(8):
        below = [[column(m[b], 8 * b0 + k) for b in range(b0 + 1, 8)] for k in range(8)]
        ahead = [column(m[b0 + 1], 8 * b0 + 8 + k) for k in range(8)] if b0 < 7 else []
        pivots = jnp.ones((8, 128), F32)
        for k in range(8):
            pivot = row(diag[k], k)
            inv = 1.0 / pivot
            rest = jnp.where(row8 > k, diag[k], 0.0) * inv
            pivots = jnp.where(row8 == k, pivot, pivots)
            pivot_row = row(m[b0], k)
            heads = {k2: row(diag[k2], k) for k2 in range(k + 1, 8)}
            for k2 in heads:
                diag[k2] = diag[k2] - rest * heads[k2]
            m[b0] = m[b0] - rest * pivot_row
            for n in range(7 - b0):
                ratio = below[k][n] * inv
                m[b0 + 1 + n] = m[b0 + 1 + n] - ratio * pivot_row
                for k2 in heads:
                    below[k2][n] = below[k2][n] - ratio * heads[k2]
                if n == 0:
                    for k2 in range(8):
                        ahead[k2] = ahead[k2] - below[k][0] * row(ratio, k2)
        scale.append(pivots)
        diag = ahead
    out = []
    for b in range(8):
        y = lax.rsqrt(scale[b])
        y = y * (1.5 - 0.5 * (scale[b] * y) * y)
        out.append(m[b] * y)
    return jnp.concatenate(out, axis=0)


def subspace(halves, core, start, g_ref):
    for here in range(2):

        @pl.when(core == here)
        def _():
            for n, (a, b) in enumerate(PAIRS):
                blk = halves[(n // 5 + here) % 2][n % 5]
                for part, value in enumerate(split3(blk)):
                    g_ref[part, a * 128 : a * 128 + 128, b * 128 : b * 128 + 128] = value
                if a != b:
                    for part, value in enumerate(split3(blk.T)):
                        g_ref[part, b * 128 : b * 128 + 128, a * 128 : a * 128 + 128] = value

    lane = lax.broadcasted_iota(jnp.int32, (R, 128), 1)

    def image(w0, w1, w2):
        t = mm(jnp.concatenate([w0, w1, w2], axis=0), g_ref[0])
        u = mm(jnp.concatenate([w0, w1], axis=0), g_ref[1])
        small = t[2 * R :] + u[R:] + mm(w0, g_ref[2])
        return t[:R] + (t[R : 2 * R] + u[:R]) + small

    def step(k, w):
        w0, w1, w2 = split3(w)
        ws = jnp.concatenate([w0, w1], axis=0)
        c = mm(ws, ws, NT)
        c = c[:R] + c[R:]
        z0, z1, z2 = split3(jnp.where(k == ITERS - 1, w, image(w0, w1, w2)))
        li = inverse_factor(c + pltpu.roll(c, R, 1))
        l0 = li.astype(BF).astype(F32)
        rest = li - l0
        l1 = rest.astype(BF).astype(F32)
        x = jnp.where(lane < R, l0, pltpu.roll(l1, R, 1)).astype(BF)
        y = jnp.where(lane < R, rest - l1, pltpu.roll(l0, R, 1)).astype(BF)
        return mm(
            jnp.concatenate([x, x, y], axis=1),
            jnp.concatenate([z0, z0, z1, z1, z0, z2], axis=0),
        )

    return lax.fori_loop(0, ITERS, step, image(*split3(start)))


def masked_factor(halves, start_ref, rank_ref, place_ref, mode, g_ref):
    v = subspace(halves, place_ref[0], start_ref[mode], g_ref)
    index = lax.broadcasted_iota(jnp.int32, (R, N), 0)
    return jnp.where(index < rank_ref[mode], v, 0.0)


def regroup_kernel(x_hbm, out_ref, sem):
    copies = [
        pltpu.make_async_copy(x_hbm.at[s, :, pl.ds(8 * g, 8), :], out_ref.at[8 * s + g], sem.at[8 * s + g])
        for s in range(4)
        for g in range(8)
    ]
    for c in copies:
        c.start()
    for c in copies:
        c.wait()


def regroup(x):
    return pl.pallas_call(
        regroup_kernel,
        out_shape=jax.ShapeDtypeStruct((32, 64, 8, 128), F32),
        in_specs=[HBM],
        out_specs=VMEM,
        scratch_shapes=[pltpu.SemaphoreType.DMA((32,))],
        compiler_params=pltpu.CompilerParams(vmem_limit_bytes=42 * 2**20),
        name="regroup",
    )(x)


def gram_one_kernel(place_ref, x_ref, keep_ref, send_ref, x2_ref, low_ref, high_ref, cross_ref):
    step = pl.program_id(0)

    @pl.when(step == 0)
    def _():
        low_ref[...] = jnp.zeros_like(low_ref)
        high_ref[...] = jnp.zeros_like(high_ref)
        cross_ref[...] = jnp.zeros_like(cross_ref)

    for p in range(0, 8, 2):
        his, los = [], []
        for k in (p, p + 1):
            parts = [split(x_ref[g, 0, pl.ds(k, 64, stride=8), :]) for g in range(8)]
            hi = jnp.concatenate([h for h, _ in parts], axis=0)
            lo = jnp.concatenate([l for _, l in parts], axis=0)
            x2_ref[0, k] = hi
            x2_ref[1, k] = lo
            his.append(hi)
            los.append(lo)
        xh = jnp.concatenate(his, axis=1)
        low_ref[...] += mm(xh[:256], xh, NT)
        high_ref[...] += mm(xh[256:], xh[256:], NT)
        cross_ref[...] += mm(xh, jnp.concatenate(los, axis=1), NT)

    @pl.when(step == pl.num_programs(0) - 1)
    def _():
        cross = cross_ref[...]
        cross = cross + cross.T
        low = low_ref[...] + cross[:256]
        high = high_ref[...] + cross[256:, 256:]
        put_blocks(keep_ref, send_ref, place_ref[0], low * 2.0**-20, high * 2.0**-20)


def gram_one(place, x):
    half = pl.BlockSpec((5, 128, 128), lambda i: (0, 0, 0))
    return pl.pallas_call(
        gram_one_kernel,
        grid=(4,),
        out_shape=(HALF, HALF, pltpu.HBM((2, 8, N, N), BF)),
        in_specs=[SMEM, pl.BlockSpec((8, 1, N, 128), lambda i: (0, i, 0, 0))],
        out_specs=(half, half, pl.BlockSpec((2, 8, N, 128), lambda i: (0, 0, 0, i))),
        scratch_shapes=[pltpu.VMEM((256, N), F32), pltpu.VMEM((256, 256), F32), pltpu.VMEM((N, N), F32)],
        compiler_params=pltpu.CompilerParams(vmem_limit_bytes=40 * 2**20),
        name="gram_one",
    )(place, x)


def factor_one_kernel(
    mine_ref, other_ref, start_ref, rank_ref, place_ref, x_hbm, u_ref, a_ref, keep_ref, send_ref, g_ref, x_ref, sem
):
    copy = pltpu.make_async_copy(x_hbm, x_ref, sem)
    copy.start()
    v = masked_factor((mine_ref, other_ref), start_ref, rank_ref, place_ref, 0, g_ref)
    u_ref[...] = v
    vh, vl = split(v)
    vs = jnp.concatenate([vh, vl], axis=0)
    copy.wait()
    for p in range(8):
        t = mm(vs, x_ref[0, p])
        y = t[:R] + t[R:] + mm(vh, x_ref[1, p])
        for q in range(4):
            a_ref[q, pl.ds(p, R, stride=8), :] = y[:, 128 * q : 128 * q + 128]
    a = jnp.concatenate([a_ref[q] for q in range(4)], axis=1)
    ah, al = split(a)
    th, tl = split(a.T)
    low = mm(th[:256], ah) + mm(th[:256], al) + mm(tl[:256], ah)
    high = mm(th[256:], ah[:, 256:]) + mm(th[256:], al[:, 256:]) + mm(tl[256:], ah[:, 256:])
    put_blocks(keep_ref, send_ref, place_ref[0], low * 2.0**-20, high * 2.0**-20)


def factor_one(halves, starts, ranks, place, x2):
    return pl.pallas_call(
        factor_one_kernel,
        out_shape=(
            jax.ShapeDtypeStruct((R, N), F32),
            jax.ShapeDtypeStruct((4, N, 128), F32),
            HALF,
            HALF,
        ),
        in_specs=[VMEM, VMEM, VMEM, SMEM, SMEM, HBM],
        out_specs=(VMEM,) * 4,
        scratch_shapes=[
            pltpu.VMEM((3, N, N), BF),
            pltpu.VMEM((2, 8, N, N), BF),
            pltpu.SemaphoreType.DMA,
        ],
        compiler_params=pltpu.CompilerParams(vmem_limit_bytes=48 * 2**20),
        name="factor_one",
    )(*halves, starts, ranks, place, x2)


def factor_two_kernel(
    mine_ref, other_ref, start_ref, rank_ref, place_ref, a_ref, u_ref, out_ref, g_ref, y_ref
):
    v = masked_factor((mine_ref, other_ref), start_ref, rank_ref, place_ref, 1, g_ref)
    u_ref[...] = v
    vh, vl = split(v)
    vs = jnp.concatenate([vh, vl], axis=0)
    ah, al = split(jnp.concatenate([a_ref[q] for q in range(4)], axis=1))
    y = mm(ah, vs, NT) + mm(al, vs, NT)
    y_ref[...] = y + pltpu.roll(y, R, 1)
    group = lax.broadcasted_iota(jnp.int32, (8, 128), 1) // 8
    for by in range(4):
        tiles = [jnp.zeros((8, 128), F32) for _ in range(8)]
        for p in range(8):
            for e in range(2):
                rows = y_ref[pl.ds(by * 128 + e * 8 + p, 8, stride=16), :]
                for bx in range(8):
                    shift = (2 * p + e - bx) % 8
                    moved = pltpu.roll(rows, 8 * shift, 1) if shift else rows
                    tiles[bx] = jnp.where(group == 2 * p + e, moved, tiles[bx])
        for bx in range(8):
            out_ref[bx * 32 + by * 8 : bx * 32 + by * 8 + 8, :] = tiles[bx]


def factor_two(halves, starts, ranks, place, a):
    return pl.pallas_call(
        factor_two_kernel,
        out_shape=(
            jax.ShapeDtypeStruct((R, N), F32),
            jax.ShapeDtypeStruct((256, 128), F32),
        ),
        in_specs=[VMEM, VMEM, VMEM, SMEM, SMEM, VMEM],
        out_specs=(VMEM, VMEM),
        scratch_shapes=[pltpu.VMEM((3, N, N), BF), pltpu.VMEM((N, 128), F32)],
        compiler_params=pltpu.CompilerParams(vmem_limit_bytes=32 * 2**20),
        name="factor_two",
    )(*halves, starts, ranks, place, a)


def gram_three_kernel(place_ref, y_ref, keep_ref, send_ref, b_ref):
    group = lax.broadcasted_iota(jnp.int32, (8, 128), 1) // 16
    for pg in range(8):
        for p in range(8):
            rows = jnp.zeros((8, 128), F32)
            for s in range(4):
                at = (8 * s + pg) * 8
                tile = y_ref[at : at + 8, :]
                if s != p:
                    tile = pltpu.roll(tile, (16 * (s - p)) % 128, 1)
                rows = jnp.where(group == s, tile, rows)
            b_ref[pl.ds(8 * pg + p, 8, stride=R), :] = rows
    bh, bl = split(b_ref[...])
    low = mm(bh[:256], bh, NT) + mm(bh[:256], bl, NT) + mm(bl[:256], bh, NT)
    high = mm(bh[256:], bh[256:], NT) + mm(bh[256:], bl[256:], NT) + mm(bl[256:], bh[256:], NT)
    put_blocks(keep_ref, send_ref, place_ref[0], low * 2.0**-20, high * 2.0**-20)


def gram_three(place, y):
    return pl.pallas_call(
        gram_three_kernel,
        out_shape=(HALF, HALF, jax.ShapeDtypeStruct((N, 128), F32)),
        in_specs=[SMEM, VMEM],
        out_specs=(VMEM, VMEM, VMEM),
        compiler_params=pltpu.CompilerParams(vmem_limit_bytes=32 * 2**20),
        name="gram_three",
    )(place, y)


def factor_three_kernel(
    mine_ref, other_ref, start_ref, rank_ref, place_ref, b_ref, u_one_ref, u_two_ref, u_ref, core_ref, g_ref
):
    v = masked_factor((mine_ref, other_ref), start_ref, rank_ref, place_ref, 2, g_ref)
    u_ref[0] = u_one_ref[...]
    u_ref[1] = u_two_ref[...]
    u_ref[2] = v
    vh, vl = split(v)
    bh, bl = split(b_ref[...])
    t = mm(jnp.concatenate([vh, vl], axis=0), bh)
    core = t[:R] + t[R:] + mm(vh, bl)
    core = jnp.concatenate([core, core], axis=0).T
    for s in range(4):
        for e in range(2):
            core_ref[s, e] = core[16 * s + 8 * e : 16 * s + 8 * e + 8, :R]


def factor_three(halves, starts, ranks, place, b, u_one, u_two):
    return pl.pallas_call(
        factor_three_kernel,
        out_shape=(
            jax.ShapeDtypeStruct((3, R, N), F32),
            jax.ShapeDtypeStruct((4, 2, 8, R), F32),
        ),
        in_specs=[VMEM, VMEM, VMEM, SMEM, SMEM, VMEM, VMEM, VMEM],
        out_specs=(VMEM, VMEM),
        scratch_shapes=[pltpu.VMEM((3, N, N), BF)],
        compiler_params=pltpu.CompilerParams(vmem_limit_bytes=32 * 2**20),
        name="factor_three",
    )(*halves, starts, ranks, place, b, u_one, u_two)


PLANE = ("y", "gy")


def swap(x, axes):
    return lax.all_to_all(x, axes, 0, 0, tiled=True)


def spread(x, axes, count):
    return swap(jnp.broadcast_to(x[None], (count,) + x.shape), axes)


def other_core(x):
    return lax.ppermute(x, "core", [(0, 1), (1, 0)])


def total(keep, send):
    g = keep + other_core(send)
    g = jnp.sum(swap(g.reshape(16, 40, 128), PLANE), axis=0)
    g = jnp.sum(spread(g, "gz", 8), axis=0)
    g = spread(g, PLANE, 16).reshape(5, 128, 128)
    return g, other_core(g)


def local(tensor, starts, trunc_ranks):
    starts_t = jnp.swapaxes(starts, 1, 2)
    place = lax.axis_index("core").astype(jnp.int32).reshape(1)
    tensor, place = lax.optimization_barrier((tensor, place))
    x = regroup(tensor).reshape(32, N, 128)
    x = swap(x, ("y", "core", "gy")).reshape(8, 4, N, 128)
    keep, send, x2 = gram_one(place, x)
    u_one, a, keep, send = factor_one(total(keep, send), starts_t, trunc_ranks, place, x2)
    u_two, y = factor_two(total(keep, send), starts_t, trunc_ranks, place, a)
    y = swap(y.reshape(256, 1, 128), ("y", "core", "gy", "gz")).reshape(256, 128)
    keep, send, b = gram_three(place, y)
    factors, core_out = factor_three(total(keep, send), starts_t, trunc_ranks, place, b, u_one, u_two)
    return (jnp.swapaxes(core_out, 2, 3), jnp.swapaxes(factors, 1, 2))


def solution(mesh):
    fine = jax.sharding.Mesh(mesh.devices.reshape(4, 2, 4, 8), ("y", "core", "gy", "gz"))
    gx = ("y", "core")
    return jax.shard_map(
        local,
        mesh=fine,
        in_specs=(P(None, gx, "gz", "gy"), P(), P()),
        out_specs=(P(None, ("gy", "gz"), None, gx), P()),
        check_vma=False,
    )
```

```python
import jax
import jax.numpy as jnp
from jax import lax
from jax.experimental import pallas as pl
from jax.experimental.pallas import tpu as pltpu
from jax.sharding import PartitionSpec as P

N = 512
R = 64
ITERS = 4
BF = jnp.bfloat16
F32 = jnp.float32
PAIRS = [(a, b) for a in range(4) for b in range(a, 4)]
NT = (((1,), (1,)), ((), ()))
NN = (((1,), (0,)), ((), ()))
VMEM = pl.BlockSpec(memory_space=pltpu.VMEM)
SMEM = pl.BlockSpec(memory_space=pltpu.SMEM)
HBM = pl.BlockSpec(memory_space=pltpu.HBM)


def split(x):
    hi = x.astype(BF)
    return hi, (x - hi.astype(F32)).astype(BF)


def split3(x):
    hi = x.astype(BF)
    rest = x - hi.astype(F32)
    mid = rest.astype(BF)
    return hi, mid, (rest - mid.astype(F32)).astype(BF)


def mm(a, b, dims=NN):
    return lax.dot_general(a, b, dims, preferred_element_type=F32)


def put_blocks(keep_ref, send_ref, core, low, high):
    for here in range(2):

        @pl.when(core == here)
        def _():
            for n, (a, b) in enumerate(PAIRS):
                out_ref = keep_ref if n // 5 == here else send_ref
                if out_ref is None:
                    continue
                if a < 2:
                    out_ref[n % 5] = low[a * 128 : a * 128 + 128, b * 128 : b * 128 + 128]
                else:
                    out_ref[n % 5] = high[a * 128 - 256 : a * 128 - 128, b * 128 - 256 : b * 128 - 128]


HALF = jax.ShapeDtypeStruct((5, 128, 128), F32)


def column(x, j):
    return jnp.broadcast_to(x[:, R + j : R + j + 1], (8, 128))


def row(x, k):
    return jnp.broadcast_to(x[k : k + 1, :], (8, 128))


def inverse_factor(cc):
    row8 = lax.broadcasted_iota(jnp.int32, (8, 128), 0)
    lane = lax.broadcasted_iota(jnp.int32, (8, 128), 1)
    m = [
        jnp.where(lane < R, (lane == row8 + 8 * b).astype(F32), cc[8 * b : 8 * b + 8, :])
        for b in range(8)
    ]
    scale = []
    diag = [column(m[0], k) for k in range(8)]
    for b0 in range(8):
        below = [[column(m[b], 8 * b0 + k) for b in range(b0 + 1, 8)] for k in range(8)]
        ahead = [column(m[b0 + 1], 8 * b0 + 8 + k) for k in range(8)] if b0 < 7 else []
        pivots = jnp.ones((8, 128), F32)
        for k in range(8):
            pivot = row(diag[k], k)
            inv = 1.0 / pivot
            rest = jnp.where(row8 > k, diag[k], 0.0) * inv
            pivots = jnp.where(row8 == k, pivot, pivots)
            pivot_row = row(m[b0], k)
            heads = {k2: row(diag[k2], k) for k2 in range(k + 1, 8)}
            for k2 in heads:
                diag[k2] = diag[k2] - rest * heads[k2]
            m[b0] = m[b0] - rest * pivot_row
            for n in range(7 - b0):
                ratio = below[k][n] * inv
                m[b0 + 1 + n] = m[b0 + 1 + n] - ratio * pivot_row
                for k2 in heads:
                    below[k2][n] = below[k2][n] - ratio * heads[k2]
                if n == 0:
                    for k2 in range(8):
                        ahead[k2] = ahead[k2] - below[k][0] * row(ratio, k2)
        scale.append(pivots)
        diag = ahead
    out = []
    for b in range(8):
        y = lax.rsqrt(scale[b])
        y = y * (1.5 - 0.5 * (scale[b] * y) * y)
        out.append(m[b] * y)
    return jnp.concatenate(out, axis=0)


def subspace(halves, core, start, g_ref):
    for here in range(2):

        @pl.when(core == here)
        def _():
            for n, (a, b) in enumerate(PAIRS):
                blk = halves[(n // 5 + here) % 2][n % 5]
                for part, value in enumerate(split3(blk)):
                    g_ref[part, a * 128 : a * 128 + 128, b * 128 : b * 128 + 128] = value
                if a != b:
                    for part, value in enumerate(split3(blk.T)):
                        g_ref[part, b * 128 : b * 128 + 128, a * 128 : a * 128 + 128] = value

    lane = lax.broadcasted_iota(jnp.int32, (R, 128), 1)

    def image(w0, w1, w2):
        t = mm(jnp.concatenate([w0, w1, w2], axis=0), g_ref[0])
        u = mm(jnp.concatenate([w0, w1], axis=0), g_ref[1])
        small = t[2 * R :] + u[R:] + mm(w0, g_ref[2])
        return t[:R] + (t[R : 2 * R] + u[:R]) + small

    def step(k, w):
        w0, w1, w2 = split3(w)
        ws = jnp.concatenate([w0, w1], axis=0)
        c = mm(ws, ws, NT)
        c = c[:R] + c[R:]
        z0, z1, z2 = split3(jnp.where(k == ITERS - 1, w, image(w0, w1, w2)))
        li = inverse_factor(c + pltpu.roll(c, R, 1))
        l0 = li.astype(BF).astype(F32)
        rest = li - l0
        l1 = rest.astype(BF).astype(F32)
        x = jnp.where(lane < R, l0, pltpu.roll(l1, R, 1)).astype(BF)
        y = jnp.where(lane < R, rest - l1, pltpu.roll(l0, R, 1)).astype(BF)
        return mm(
            jnp.concatenate([x, x, y], axis=1),
            jnp.concatenate([z0, z0, z1, z1, z0, z2], axis=0),
        )

    return lax.fori_loop(0, ITERS, step, image(*split3(start)))


def masked_factor(halves, start_ref, rank_ref, place_ref, mode, g_ref):
    v = subspace(halves, place_ref[0], start_ref[mode], g_ref)
    index = lax.broadcasted_iota(jnp.int32, (R, N), 0)
    return jnp.where(index < rank_ref[mode], v, 0.0)


def regroup_kernel(x_hbm, out_ref, sem):
    copies = [
        pltpu.make_async_copy(x_hbm.at[s, :, pl.ds(8 * g, 8), :], out_ref.at[8 * s + g], sem.at[8 * s + g])
        for s in range(4)
        for g in range(8)
    ]
    for c in copies:
        c.start()
    for c in copies:
        c.wait()


def regroup(x):
    return pl.pallas_call(
        regroup_kernel,
        out_shape=jax.ShapeDtypeStruct((32, 64, 8, 128), F32),
        in_specs=[HBM],
        out_specs=VMEM,
        scratch_shapes=[pltpu.SemaphoreType.DMA((32,))],
        compiler_params=pltpu.CompilerParams(vmem_limit_bytes=42 * 2**20),
        name="regroup",
    )(x)


def gram_one_kernel(place_ref, x_ref, keep_ref, send_ref, x2_ref, low_ref, high_ref, cross_ref):
    step = pl.program_id(0)

    @pl.when(step == 0)
    def _():
        low_ref[...] = jnp.zeros_like(low_ref)
        high_ref[...] = jnp.zeros_like(high_ref)
        cross_ref[...] = jnp.zeros_like(cross_ref)

    for p in range(0, 8, 2):
        his, los = [], []
        for k in (p, p + 1):
            parts = [split(x_ref[g, 0, pl.ds(k, 64, stride=8), :]) for g in range(8)]
            hi = jnp.concatenate([h for h, _ in parts], axis=0)
            lo = jnp.concatenate([l for _, l in parts], axis=0)
            x2_ref[0, k] = hi
            x2_ref[1, k] = lo
            his.append(hi)
            los.append(lo)
        xh = jnp.concatenate(his, axis=1)
        low_ref[...] += mm(xh[:256], xh, NT)
        high_ref[...] += mm(xh[256:], xh[256:], NT)
        cross_ref[...] += mm(xh, jnp.concatenate(los, axis=1), NT)

    @pl.when(step == pl.num_programs(0) - 1)
    def _():
        cross = cross_ref[...]
        cross = cross + cross.T
        low = low_ref[...] + cross[:256]
        high = high_ref[...] + cross[256:, 256:]
        put_blocks(keep_ref, send_ref, place_ref[0], low * 2.0**-20, high * 2.0**-20)


def gram_one(place, x):
    half = pl.BlockSpec((5, 128, 128), lambda i: (0, 0, 0))
    return pl.pallas_call(
        gram_one_kernel,
        grid=(4,),
        out_shape=(HALF, HALF, pltpu.HBM((2, 8, N, N), BF)),
        in_specs=[SMEM, pl.BlockSpec((8, 1, N, 128), lambda i: (0, i, 0, 0))],
        out_specs=(half, half, pl.BlockSpec((2, 8, N, 128), lambda i: (0, 0, 0, i))),
        scratch_shapes=[pltpu.VMEM((256, N), F32), pltpu.VMEM((256, 256), F32), pltpu.VMEM((N, N), F32)],
        compiler_params=pltpu.CompilerParams(vmem_limit_bytes=40 * 2**20),
        name="gram_one",
    )(place, x)


def factor_one_kernel(
    mine_ref, other_ref, start_ref, rank_ref, place_ref, x_hbm, u_ref, a_ref, keep_ref, send_ref, g_ref, x_ref, sem
):
    copy = pltpu.make_async_copy(x_hbm, x_ref, sem)
    copy.start()
    v = masked_factor((mine_ref, other_ref), start_ref, rank_ref, place_ref, 0, g_ref)
    u_ref[...] = v
    vh, vl = split(v)
    vs = jnp.concatenate([vh, vl], axis=0)
    copy.wait()
    for p in range(8):
        t = mm(vs, x_ref[0, p])
        y = t[:R] + t[R:] + mm(vh, x_ref[1, p])
        for q in range(4):
            a_ref[q, pl.ds(p, R, stride=8), :] = y[:, 128 * q : 128 * q + 128]
    a = jnp.concatenate([a_ref[q] for q in range(4)], axis=1)
    ah, al = split(a)
    th, tl = split(a.T)
    low = mm(th[:256], ah) + mm(th[:256], al) + mm(tl[:256], ah)
    high = mm(th[256:], ah[:, 256:]) + mm(th[256:], al[:, 256:]) + mm(tl[256:], ah[:, 256:])
    put_blocks(keep_ref, send_ref, place_ref[0], low * 2.0**-20, high * 2.0**-20)


def factor_one(halves, starts, ranks, place, x2):
    return pl.pallas_call(
        factor_one_kernel,
        out_shape=(
            jax.ShapeDtypeStruct((R, N), F32),
            jax.ShapeDtypeStruct((4, N, 128), F32),
            HALF,
            HALF,
        ),
        in_specs=[VMEM, VMEM, VMEM, SMEM, SMEM, HBM],
        out_specs=(VMEM,) * 4,
        scratch_shapes=[
            pltpu.VMEM((3, N, N), BF),
            pltpu.VMEM((2, 8, N, N), BF),
            pltpu.SemaphoreType.DMA,
        ],
        compiler_params=pltpu.CompilerParams(vmem_limit_bytes=48 * 2**20),
        name="factor_one",
    )(*halves, starts, ranks, place, x2)


def factor_two_kernel(
    mine_ref, other_ref, start_ref, rank_ref, place_ref, a_ref, u_ref, out_ref, g_ref, y_ref
):
    v = masked_factor((mine_ref, other_ref), start_ref, rank_ref, place_ref, 1, g_ref)
    u_ref[...] = v
    vh, vl = split(v)
    vs = jnp.concatenate([vh, vl], axis=0)
    ah, al = split(jnp.concatenate([a_ref[q] for q in range(4)], axis=1))
    y = mm(ah, vs, NT) + mm(al, vs, NT)
    y_ref[...] = y + pltpu.roll(y, R, 1)
    group = lax.broadcasted_iota(jnp.int32, (8, 128), 1) // 8
    for by in range(4):
        tiles = [jnp.zeros((8, 128), F32) for _ in range(8)]
        for p in range(8):
            for e in range(2):
                rows = y_ref[pl.ds(by * 128 + e * 8 + p, 8, stride=16), :]
                for bx in range(8):
                    shift = (2 * p + e - bx) % 8
                    moved = pltpu.roll(rows, 8 * shift, 1) if shift else rows
                    tiles[bx] = jnp.where(group == 2 * p + e, moved, tiles[bx])
        for bx in range(8):
            out_ref[bx * 32 + by * 8 : bx * 32 + by * 8 + 8, :] = tiles[bx]


def factor_two(halves, starts, ranks, place, a):
    return pl.pallas_call(
        factor_two_kernel,
        out_shape=(
            jax.ShapeDtypeStruct((R, N), F32),
            jax.ShapeDtypeStruct((256, 128), F32),
        ),
        in_specs=[VMEM, VMEM, VMEM, SMEM, SMEM, VMEM],
        out_specs=(VMEM, VMEM),
        scratch_shapes=[pltpu.VMEM((3, N, N), BF), pltpu.VMEM((N, 128), F32)],
        compiler_params=pltpu.CompilerParams(vmem_limit_bytes=32 * 2**20),
        name="factor_two",
    )(*halves, starts, ranks, place, a)


def gram_three_kernel(place_ref, y_ref, other_ref, keep_ref, b_ref):
    group = lax.broadcasted_iota(jnp.int32, (8, 128), 1) // 16
    for pg in range(8):
        for p in range(8):
            rows = jnp.zeros((8, 128), F32)
            for g in range(8):
                at = (8 * (g % 4) + pg) * 8
                tile = (y_ref if g < 4 else other_ref)[at : at + 8, :]
                if g != p:
                    tile = pltpu.roll(tile, (16 * (g - p)) % 128, 1)
                rows = jnp.where(group == g, tile, rows)
            b_ref[pl.ds(8 * pg + p, 8, stride=R), :] = rows
    bh, bl = split(b_ref[...])
    low = mm(bh[:256], bh, NT) + mm(bh[:256], bl, NT) + mm(bl[:256], bh, NT)
    high = mm(bh[256:], bh[256:], NT) + mm(bh[256:], bl[256:], NT) + mm(bl[256:], bh[256:], NT)
    put_blocks(keep_ref, None, place_ref[0], low * 2.0**-20, high * 2.0**-20)


def gram_three(place, y, other):
    return pl.pallas_call(
        gram_three_kernel,
        out_shape=(HALF, jax.ShapeDtypeStruct((N, 128), F32)),
        in_specs=[SMEM, VMEM, VMEM],
        out_specs=(VMEM, VMEM),
        compiler_params=pltpu.CompilerParams(vmem_limit_bytes=32 * 2**20),
        name="gram_three",
    )(place, y, other)


def factor_three_kernel(
    mine_ref, other_ref, start_ref, rank_ref, place_ref, b_ref, u_one_ref, u_two_ref, u_ref, core_ref, g_ref
):
    v = masked_factor((mine_ref, other_ref), start_ref, rank_ref, place_ref, 2, g_ref)
    u_ref[0] = u_one_ref[...]
    u_ref[1] = u_two_ref[...]
    u_ref[2] = v
    vh, vl = split(v)
    bh, bl = split(b_ref[...])
    t = mm(jnp.concatenate([vh, vl], axis=0), bh)
    core = t[:R] + t[R:] + mm(vh, bl)
    core = jnp.concatenate([core, core], axis=0).T
    for s in range(4):
        for e in range(2):
            core_ref[s, e] = core[16 * s + 8 * e : 16 * s + 8 * e + 8, :R]


def factor_three(halves, starts, ranks, place, b, u_one, u_two):
    return pl.pallas_call(
        factor_three_kernel,
        out_shape=(
            jax.ShapeDtypeStruct((3, R, N), F32),
            jax.ShapeDtypeStruct((4, 2, 8, R), F32),
        ),
        in_specs=[VMEM, VMEM, VMEM, SMEM, SMEM, VMEM, VMEM, VMEM],
        out_specs=(VMEM, VMEM),
        scratch_shapes=[pltpu.VMEM((3, N, N), BF)],
        compiler_params=pltpu.CompilerParams(vmem_limit_bytes=32 * 2**20),
        name="factor_three",
    )(*halves, starts, ranks, place, b, u_one, u_two)


PLANE = ("y", "gy")


def swap(x, axes):
    return lax.all_to_all(x, axes, 0, 0, tiled=True)


def spread(x, axes, count):
    return swap(jnp.broadcast_to(x[None], (count,) + x.shape), axes)


def other_core(x):
    return lax.ppermute(x, "core", [(0, 1), (1, 0)])


def total(g):
    g = jnp.sum(swap(g.reshape(16, 40, 128), PLANE), axis=0)
    g = jnp.sum(spread(g, "gz", 8), axis=0)
    g = spread(g, PLANE, 16).reshape(5, 128, 128)
    return g, other_core(g)


def local(tensor, starts, trunc_ranks):
    starts_t = jnp.swapaxes(starts, 1, 2)
    place = lax.axis_index("core").astype(jnp.int32).reshape(1)
    tensor, place = lax.optimization_barrier((tensor, place))
    x = regroup(tensor).reshape(32, N, 128)
    x = swap(x, ("y", "core", "gy")).reshape(8, 4, N, 128)
    keep, send, x2 = gram_one(place, x)
    u_one, a, keep, send = factor_one(total(keep + other_core(send)), starts_t, trunc_ranks, place, x2)
    u_two, y = factor_two(total(keep + other_core(send)), starts_t, trunc_ranks, place, a)
    y = swap(y.reshape(256, 1, 128), ("y", "core", "gy", "gz")).reshape(256, 128)
    g, b = gram_three(place, y, other_core(y))
    factors, core_out = factor_three(total(g), starts_t, trunc_ranks, place, b, u_one, u_two)
    return (jnp.swapaxes(core_out, 2, 3), jnp.swapaxes(factors, 1, 2))


def solution(mesh):
    fine = jax.sharding.Mesh(mesh.devices.reshape(4, 2, 4, 8), ("y", "core", "gy", "gz"))
    gx = ("y", "core")
    return jax.shard_map(
        local,
        mesh=fine,
        in_specs=(P(None, gx, "gz", "gy"), P(), P()),
        out_specs=(P(None, ("gy", "gz"), None, gx), P()),
        check_vma=False,
    )
```
